256 devices in a mesh: brick: 64 (over x, y_lo, z), row: 4 (over y_hi, core).
Axes of the slice: x: 4, y: 4 (y_hi: 2, y_lo: 2; y = y_hi * 2 + y_lo), z: 8, core: 2. Of those that a mesh axis runs over, the one named last changes fastest.
Arguments:
- magnet: float32 [3, 512, 128, 256], P(None, 'brick', 'row'), may hold values from -6 to 6
- node_position: float32 [3, 98304], replicated, may hold values from 0 to 8
- node_moment: float32 [3, 98304], replicated, may hold values from -5 to 5
- solid_fraction: float32 [98304], replicated, may hold values from 0.3 to 0.7
- request_cell: int32 [64, 4, 64, 12], P('brick', 'row'), may hold values from 0 to 65535, as said below
- request_slot: int32 [64, 4, 64, 12], P('brick', 'row'), may hold values from 0 to 1535, as said below
- request_count: int32 [64, 4, 64], P('brick', 'row'), may hold values from 0 to 12, as said below
Outputs:
- potential: float32 [512, 128, 256], P('brick', 'row')
- boundary_u2: float32 [64, 4, 64, 12], P('brick', 'row')
The draws below stay inside these ranges and needn't reach their ends.
Inputs may be any that keep to these rules, and one draw needn't show every extreme that they name: `request_count`: over all devices, the counts toward one column block sum to 1536; some device's count is exactly 12 in every column block. `request_slot`: over all devices, the live slots toward column block b name each of its 1536 positions exactly once; dead slots hold arbitrary positions. `request_cell`: the live slots of one device name distinct cells.
All inputs are finite; a program needn't handle non-finite values.
Results may differ from the reference program's by a relative error of at most 0.0003.
Values sent between devices are 32-bit elements; how exact they have to be, the bound alone decides.
No kernel may reach another device: no remote copies, remote signals or barrier semaphores. Data moves between devices by JAX's collectives and lax.ppermute only.
A program may use at most 64 MiB of HBM per device.

```python
import math
import jax
import jax.numpy as jnp
from jax import lax

CX = 8
CY = 32
CZ = 256
SWEEPS = 12
NX = 512
NY = 128
NODES = 98304
BLOCK = 1536
CAP = 12
N_BRICK = 64
N_ROW = 4


def one_permutation(subkey):
    return jax.random.permutation(subkey, N_BRICK * N_ROW).astype(jnp.int32)


def block_permutation(subkey):
    return jax.random.permutation(subkey, BLOCK).astype(jnp.int32)


def routing_tables(key):
    base = jax.random.fold_in(key, 7)
    key_list = jax.random.split(base, 4)
    senders = N_BRICK * N_ROW
    lengths = jax.random.randint(key_list[0], (N_BRICK, senders), CAP // 2, CAP + 1).astype(jnp.int32)
    lengths = lengths.at[:, 0].set(CAP)
    run_ends = jnp.cumsum(lengths, axis=1)
    run_starts = run_ends - lengths
    run_counts = jnp.minimum(run_ends, BLOCK) - jnp.minimum(run_starts, BLOCK)
    owner_of_run = jax.vmap(one_permutation)(jax.random.split(key_list[1], N_BRICK))
    run_of_owner = jnp.argsort(owner_of_run, axis=1).astype(jnp.int32)
    counts = jnp.take_along_axis(run_counts, run_of_owner, axis=1)
    begins = jnp.take_along_axis(run_starts, run_of_owner, axis=1)
    node_order = jax.vmap(block_permutation)(jax.random.split(key_list[2], N_BRICK))
    slot_range = jnp.arange(CAP).astype(jnp.int32)
    picks = jnp.minimum(begins[:, :, None] + slot_range[None, None, :], BLOCK - 1)
    slots = jnp.take_along_axis(node_order, picks.reshape(N_BRICK, senders * CAP), axis=1).reshape(N_BRICK, senders, CAP)
    stride = CX * CY * CZ // (N_BRICK * CAP)
    jitter = jax.random.randint(key_list[3], (N_BRICK, senders, CAP), 0, stride).astype(jnp.int32)
    brick_range = jnp.arange(N_BRICK).astype(jnp.int32)
    cells = (brick_range[:, None, None] * CAP + slot_range[None, None, :]) * stride + jitter
    cells = cells.transpose(1, 0, 2).reshape(N_BRICK, N_ROW, N_BRICK, CAP)
    slots = slots.transpose(1, 0, 2).reshape(N_BRICK, N_ROW, N_BRICK, CAP)
    counts = counts.transpose(1, 0).reshape(N_BRICK, N_ROW, N_BRICK)
    return (cells, slots, counts)


def draw_request_cell(key, part):
    return routing_tables(key)[0]


def draw_request_slot(key, part):
    return routing_tables(key)[1]


def draw_request_count(key, part):
    return routing_tables(key)[2]


def shard_levels(stream_key, shape, shards, smallest, largest):
    factor_of, own = 1.0, jax.random.fold_in(stream_key, 6)
    for dim, shards_of in shards:
        draws = jnp.exp(jax.random.uniform(jax.random.fold_in(own, dim), (shards_of,), jnp.float32, smallest / len(shards), largest / len(shards)))
        factor_of = factor_of * jnp.repeat(draws, shape[dim] // shards_of).reshape([-1 if axis == dim else 1 for axis in range(len(shape))])
    return factor_of


def normal_values(own_key, shape, deviation, reach, cuts=(), held_as=jnp.bfloat16):
    entries = jax.random.normal(own_key, shape, jnp.float32) * deviation
    if len(cuts) > 0:
        entries = shard_levels(own_key, shape, cuts, -0.22, 0.18) * entries
    return jnp.clip(entries, min=-reach, max=reach).astype(held_as)


def setup_inputs(seed: int = 0) -> dict:
    seeds = jax.random.split(jax.random.key(seed), 8)
    magnet = normal_values(seeds[0], (3, NX, NY, CZ), 1.0, 6.0, ((1, 64), (2, 4)), jnp.float32)
    node_position = jnp.clip(jax.random.uniform(seeds[1], (3, NODES), jnp.float32, 0.0, 8.0), 0.0, 8.0)
    node_moment = normal_values(seeds[2], (3, NODES), 1.0, 5.0, (), jnp.float32)
    solid_fraction = jnp.clip(jax.random.uniform(seeds[3], (NODES,), jnp.float32, 0.3, 0.7), 0.3, 0.7)
    request_cell = draw_request_cell(jax.random.fold_in(seeds[7], 71), 0)
    request_slot = draw_request_slot(jax.random.fold_in(seeds[7], 71), 0)
    request_count = draw_request_count(jax.random.fold_in(seeds[7], 71), 0)
    return {"magnet": magnet, "node_position": node_position, "node_moment": node_moment, "solid_fraction": solid_fraction, "request_cell": request_cell, "request_slot": request_slot, "request_count": request_count}


RELAX_LOW = 0.5
RELAX_HIGH = 2.0
SOFTENING = 0.5

def sweep_weights(total_steps):
    centre = 0.5 * (RELAX_HIGH + RELAX_LOW)
    radius = 0.5 * (RELAX_HIGH - RELAX_LOW)
    root_list = [1.0 / (centre + radius * math.cos(math.pi * (2 * order_index + 1) / (2 * total_steps))) for order_index in range(total_steps)]
    ordered = []
    for order_index in range(total_steps // 2):
        ordered.append(root_list[order_index])
        ordered.append(root_list[total_steps - 1 - order_index])
    if total_steps % 2 == 1:
        ordered.append(root_list[total_steps // 2])
    return ordered

def shift_depth(planes):
    zeros_plane = jnp.zeros(planes.shape[:2] + (1,), planes.dtype)
    upward = jnp.concatenate([planes[:, :, 1:], zeros_plane], axis=2)
    downward = jnp.concatenate([zeros_plane, planes[:, :, :-1]], axis=2)
    return (upward, downward)

def beside_sum(padded):
    centre = padded[1:-1, 1:-1]
    upward, downward = shift_depth(centre)
    neighbours = padded[2:, 1:-1] + padded[:-2, 1:-1] + padded[1:-1, 2:] + padded[1:-1, :-2] + upward + downward
    return (centre, neighbours)

def divergence(padded):
    along_x = padded[0, 2:, 1:-1] - padded[0, :-2, 1:-1]
    along_y = padded[1, 1:-1, 2:] - padded[1, 1:-1, :-2]
    upward, downward = shift_depth(padded[2, 1:-1, 1:-1])
    return -0.5 * (along_x + along_y + (upward - downward))

def relax(centre, neighbours, source, weight):
    return centre + weight * (source - 6.0 * centre + neighbours) / 6.0

def double_layer(targets, sources, moments):
    delta_x = targets[0][:, None] - sources[0][None, :]
    delta_y = targets[1][:, None] - sources[1][None, :]
    delta_z = targets[2][:, None] - sources[2][None, :]
    distance_sq = delta_x * delta_x + delta_y * delta_y + delta_z * delta_z + SOFTENING
    facing = moments[0][None, :] * delta_x + moments[1][None, :] * delta_y + moments[2][None, :] * delta_z
    return facing / (4.0 * math.pi * distance_sq * jnp.sqrt(distance_sq))

def to_devices(volume):
    return volume.reshape(N_BRICK, CX, N_ROW, CY, CZ).transpose(0, 2, 1, 3, 4).reshape(N_BRICK, N_ROW, CX * CY * CZ)

def from_devices(blocks):
    return blocks.reshape(N_BRICK, N_ROW, CX, CY, CZ).transpose(0, 2, 1, 3, 4).reshape(CX * N_BRICK, CY * N_ROW, CZ)

def place_values(indices, values):
    return jnp.zeros((CX * CY * CZ,), values.dtype).at[indices].set(values, mode='drop')

def reference(magnet, node_position, node_moment, solid_fraction, request_cell, request_slot, request_count):
    weights = sweep_weights(SWEEPS)
    source = divergence(jnp.pad(magnet, ((0, 0), (1, 1), (1, 1), (0, 0))))
    first_field = jnp.zeros_like(source)
    for weight in weights:
        centre, neighbours = beside_sum(jnp.pad(first_field, ((1, 1), (1, 1), (0, 0))))
        first_field = relax(centre, neighbours, source, weight)
    cap_slots = request_cell.shape[3]
    live_slot = jnp.arange(cap_slots).astype(jnp.int32)[None, None, None, :] < request_count[..., None]
    flat_cells = request_cell.reshape(N_BRICK, N_ROW, N_BRICK * cap_slots)
    traces = jnp.take_along_axis(to_devices(first_field), flat_cells, axis=2).reshape(request_cell.shape)
    traces = jnp.where(live_slot, traces, 0.0)
    node_ids = jnp.arange(N_BRICK).astype(jnp.int32)[None, None, :, None] * BLOCK + request_slot
    drop_ids = jnp.where(live_slot, node_ids, NODES).reshape(-1)
    node_trace = jnp.zeros((NODES,), traces.dtype).at[drop_ids].add(traces.reshape(-1), mode='drop')
    row_block = math.gcd(NODES, 256)

    def layer_rows(row_start):
        targets = lax.dynamic_slice_in_dim(node_position, row_start, row_block, 1)
        kernel_tile = double_layer(targets, node_position, node_moment)
        return jnp.dot(kernel_tile, node_trace, precision=lax.Precision.HIGHEST)
    row_starts = jnp.arange(NODES // row_block).astype(jnp.int32) * row_block
    layer_value = lax.map(layer_rows, row_starts).reshape(-1)
    node_value = layer_value + (solid_fraction - 1.0) * node_trace
    safe_ids = jnp.where(live_slot, node_ids, 0).reshape(-1)
    boundary = jnp.where(live_slot, jnp.take(node_value, safe_ids).reshape(request_cell.shape), 0.0)
    clamp_index = jnp.where(live_slot, request_cell, CX * CY * CZ).reshape(N_BRICK, N_ROW, N_BRICK * cap_slots)
    placer = jax.vmap(jax.vmap(place_values))
    clamp_values = from_devices(placer(clamp_index, boundary.reshape(N_BRICK, N_ROW, N_BRICK * cap_slots)))
    clamp_mask = from_devices(placer(clamp_index, jnp.ones(clamp_index.shape, boundary.dtype))) > 0.5
    second_field = jnp.where(clamp_mask, clamp_values, 0.0)
    for weight in weights:
        centre, neighbours = beside_sum(jnp.pad(second_field, ((1, 1), (1, 1), (0, 0))))
        second_field = jnp.where(clamp_mask, clamp_values, relax(centre, neighbours, 0.0, weight))
    return (first_field + second_field, boundary)
```

```python
import functools
import math

import jax
import jax.numpy as jnp
from jax import lax
from jax.experimental import pallas as pl
from jax.experimental.pallas import tpu as pltpu
from jax.sharding import PartitionSpec as P

CX = 8
CY = 32
CZ = 256
SWEEPS = 12
CAP = 12
RELAX_LOW = 0.5
RELAX_HIGH = 2.0
SOFTENING = 0.5

YO = 12
YE = CY + 24
XS = CX + 22
XD = CX + 24
HALF = 128
PARAMS = pltpu.CompilerParams(vmem_limit_bytes=50 * 1024 * 1024)
DEAD_SLOT = 4096
TINY = 1e-30
F32 = jnp.float32
BF16 = jnp.bfloat16
VMEM = pl.BlockSpec(memory_space=pltpu.VMEM)
SMEM = pl.BlockSpec(memory_space=pltpu.SMEM)


def sweep_weights(total_steps):
    centre = 0.5 * (RELAX_HIGH + RELAX_LOW)
    radius = 0.5 * (RELAX_HIGH - RELAX_LOW)
    root_list = [
        1.0 / (centre + radius * math.cos(math.pi * (2 * order_index + 1) / (2 * total_steps)))
        for order_index in range(total_steps)
    ]
    ordered = []
    for order_index in range(total_steps // 2):
        ordered.append(root_list[order_index])
        ordered.append(root_list[total_steps - 1 - order_index])
    return ordered


WEIGHTS = sweep_weights(SWEEPS)


def shaped(*dims, dtype=F32):
    return jax.ShapeDtypeStruct(dims, dtype)


def split3(v):
    hi = v.astype(BF16).astype(F32)
    rest = v - hi
    mid = rest.astype(BF16).astype(F32)
    return hi, mid, rest - mid


def z_pair(left, right):
    lane = lax.broadcasted_iota(jnp.int32, left.shape, 1)
    left_dn = pltpu.roll(left, 1, 1)
    right_dn = pltpu.roll(right, 1, 1)
    left_up = pltpu.roll(left, HALF - 1, 1)
    right_up = pltpu.roll(right, HALF - 1, 1)
    first, last = lane == 0, lane == HALF - 1
    dn = (jnp.where(first, 0.0, left_dn), jnp.where(first, left_dn, right_dn))
    up = (jnp.where(last, right_up, left_up), jnp.where(last, 0.0, right_up))
    return dn, up


def source_kernel(m_ref, e_ref, low_ref, high_ref, pad):
    pad[...] = jnp.zeros_like(pad)
    for x in range(CX):
        pad[0, x + 1, 12:44, :] = m_ref[0, x]
        pad[1, x + 1, 12:44, :] = m_ref[1, x]
        pad[2, x + 1, 12:44, :] = m_ref[2, x]
    zeros = jnp.zeros((40, CZ), F32)
    for i in range(CX + 2):
        ahead = pad[0, i + 1, 8:48, :] if i + 1 <= CX else zeros
        behind = pad[0, i - 1, 8:48, :] if i >= 2 else zeros
        total = ahead - behind
        if 1 <= i <= CX:
            total = total + (pad[1, i, 9:49, :] - pad[1, i, 7:47, :])
            c = pad[2, i, 8:48, :]
            dn, up = z_pair(c[:, :HALF], c[:, HALF:])
            total = total + jnp.concatenate([up[0] - dn[0], up[1] - dn[1]], axis=1)
        total = -0.5 * total
        e_ref[i] = total
        if i < 4:
            low_ref[i] = total
        if i >= CX - 2:
            high_ref[i - (CX - 2)] = total


def own_source(magnet):
    return pl.pallas_call(
        source_kernel,
        out_shape=(shaped(10, 40, CZ), shaped(4, 40, CZ), shaped(4, 40, CZ)),
        in_specs=[VMEM],
        out_specs=(VMEM, VMEM, VMEM),
        scratch_shapes=[pltpu.VMEM((3, CX + 2, 56, CZ), F32)],
        compiler_params=PARAMS,
        name="own_source",
    )(magnet)


def join_kernel(e_ref, l1_ref, r1_ref, l2_ref, r2_ref, sx_ref, upper_ref, lower_ref):
    parts = ((e_ref, 10, 10), (l1_ref, 2, 10), (r1_ref, 18, 10), (l2_ref, 0, 4), (r2_ref, 26, 4))
    for plane in range(XS):
        total = None
        for ref, begin, count in parts:
            if begin <= plane < begin + count:
                term = ref[plane - begin]
                total = term if total is None else total + term
        sx_ref[plane] = total
        upper_ref[plane] = total[24:40]
        lower_ref[plane] = total[0:16]


def join_x(own, l1, r1, l2, r2):
    return pl.pallas_call(
        join_kernel,
        out_shape=(shaped(XS, 40, CZ), shaped(XS, 16, CZ), shaped(XS, 16, CZ)),
        in_specs=[VMEM] * 5,
        out_specs=(VMEM,) * 3,
        compiler_params=PARAMS,
        name="join_x",
    )(own, l1, r1, l2, r2)


def neighbours(src, x):
    c = src[x]
    around_x = src[x - 1] + src[x + 1]
    halves = (c[:, :HALF], c[:, HALF:])
    dn, up = z_pair(*halves)
    out = []
    for h in range(2):
        v = halves[h]
        around_y = pltpu.roll(v, 1, 0) + pltpu.roll(v, YE - 1, 0)
        around = around_x[:, h * HALF : (h + 1) * HALF] + around_y + (dn[h] + up[h])
        out.append((v, around))
    return out


def first_kernel(place_ref, sx_ref, below_ref, above_ref, cell_ref, base_ref, field_ref, msg_ref, s, buf):
    brick, row = place_ref[0], place_ref[1]
    cells_x, cells_y = place_ref[2], place_ref[3]
    y_at = lax.broadcasted_iota(jnp.int32, (YE, HALF), 0) + (row * CY - YO)
    in_y = jnp.where((y_at >= 0) & (y_at < cells_y), 1.0, 0.0).astype(F32)

    def x_scale(x, scale):
        at = brick * CX + x - 11
        return jnp.where((at >= 0) & (at < cells_x), scale, 0.0).astype(F32)

    def gather_plane(x, carry):
        t = sx_ref[x]
        lo = below_ref[x]
        hi = above_ref[x]
        full = jnp.concatenate(
            [lo[0:8], t[0:8] + lo[8:16], t[8:32], t[32:40] + hi[0:8], hi[8:16]], axis=0
        )
        s[x] = full
        coef = in_y * x_scale(x, WEIGHTS[0] / 6.0)
        buf[0, x, :, :HALF] = coef * full[:, :HALF]
        buf[0, x, :, HALF:] = coef * full[:, HALF:]
        return carry

    lax.fori_loop(0, XS, gather_plane, 0)
    for k in range(1, SWEEPS):
        weight = WEIGHTS[k]
        src, dst = buf.at[(k - 1) % 2], buf.at[k % 2]

        def plane(x, carry, src=src, dst=dst, weight=weight):
            coef = in_y * x_scale(x, weight / 6.0)
            source = s[x]
            for h, (v, around) in enumerate(neighbours(src, x)):
                lanes = slice(h * HALF, (h + 1) * HALF)
                dst[x, :, lanes] = (1.0 - weight) * v + coef * (source[:, lanes] + around)
            return carry

        lax.fori_loop(k, XS - k, plane, 0)
    last = (SWEEPS - 1) % 2
    for x in range(CX):
        field_ref[x] = buf[last, x + 11, YO : YO + CY, :]
    flat = field_ref[...].reshape(CX * CY, CZ)
    turned = flat.T
    parts = [p.astype(BF16) for p in split3(turned)]
    row_at = lax.broadcasted_iota(jnp.int32, (CX * CY, HALF), 0)
    picked = []
    for k in range(6):
        cell = cell_ref[k : k + 1, :]
        hot = jnp.where(row_at == (cell >> 8), 1.0, 0.0).astype(BF16)
        at_rows = sum(jnp.dot(p, hot, preferred_element_type=F32) for p in parts)
        kept = jnp.where(row_at == (cell & 255), at_rows, 0.0)
        picked.append(jnp.sum(kept, axis=0, keepdims=True))
    sub = lax.broadcasted_iota(jnp.int32, (HALF, HALF), 0)
    tile = jnp.zeros((HALF, HALF), F32)
    for k in range(6):
        tile = jnp.where(sub == k, picked[k], tile)
    turned_tile = tile.T
    both = turned_tile[0:64] + pltpu.roll(turned_tile[64:128], 6, 1)
    traces = pltpu.roll(both, CAP, 1)
    lanes = 3 * CAP
    full = base_ref[...] + traces[:, :lanes]
    for q in range(4):
        msg_ref[q] = full


def first_solve(place, sx, below, above, cells, base):
    return pl.pallas_call(
        first_kernel,
        out_shape=(shaped(CX, CY, CZ), shaped(4, 64, 3 * CAP)),
        in_specs=[SMEM] + [VMEM] * 5,
        out_specs=(VMEM, VMEM),
        scratch_shapes=[pltpu.VMEM((XS, YE, CZ), F32), pltpu.VMEM((2, XS, YE, CZ), F32)],
        compiler_params=PARAMS,
        name="first_solve",
    )(place, sx, below, above, cells, base)


def place_kernel(place_ref, got_ref, out_ref):
    row = place_ref[1]
    got = got_ref[...]
    at = (lax.broadcasted_iota(jnp.int32, (256, 384), 1) + row * 384).astype(F32)
    acc = jnp.zeros((256, 384), F32)
    for i in range(CAP):
        slot = got[:, i : i + 1]
        trace = got[:, CAP + i : CAP + i + 1]
        acc = acc + jnp.where(at == slot, trace, 0.0)
    total = jnp.sum(acc, axis=0, keepdims=True)
    out_ref[...] = jnp.broadcast_to(total, (64, 384))


def place_quarter(place, got):
    return pl.pallas_call(
        place_kernel,
        out_shape=shaped(64, 384),
        in_specs=[SMEM, VMEM],
        out_specs=VMEM,
        compiler_params=PARAMS,
        name="place_quarter",
    )(place, got)


SRC = 24576
CHUNK = 768
TILE = 128


def stack_six(v, order):
    parts = split3(v)
    return jnp.concatenate([parts[i] for i in order], axis=0)


RIGHT = (0, 1, 2, 0, 1, 0)
LEFT = (0, 0, 0, 1, 1, 2)


def prepare_kernel(target_ref, source_ref, left_ref, right_ref, moment_ref):
    sub = lax.broadcasted_iota(jnp.int32, (8, CHUNK), 0)

    def sources(c, carry):
        at = pl.multiple_of(c * CHUNK, CHUNK)
        v = source_ref[:, pl.ds(at, CHUNK)]
        pos = v[0:3] - 4.0
        mom = v[3:6]
        norm = jnp.sum(pos * pos, axis=0, keepdims=True)
        across = jnp.sum(pos * mom, axis=0, keepdims=True)
        dist = jnp.where(sub == 3, 1.0, jnp.where(sub == 4, norm, 0.0))
        face = jnp.where(sub == 4, -across, 0.0)
        for i in range(3):
            dist = jnp.where(sub == i, -2.0 * pos[i : i + 1], dist)
            face = jnp.where(sub == i, mom[i : i + 1], face)
        right_ref[:, pl.ds(at, CHUNK)] = stack_six(dist, RIGHT).astype(BF16)
        moment_ref[:, pl.ds(at, CHUNK)] = face
        return carry

    lax.fori_loop(0, SRC // CHUNK, sources, 0)
    sub = lax.broadcasted_iota(jnp.int32, (8, TILE), 0)
    for t in range(1536 // TILE):
        pos = target_ref[0:3, t * TILE : (t + 1) * TILE] - 4.0
        norm = jnp.sum(pos * pos, axis=0, keepdims=True) + SOFTENING
        feat = jnp.where(sub == 3, norm, jnp.where(sub == 4, 1.0, 0.0))
        for i in range(3):
            feat = jnp.where(sub == i, pos[i : i + 1], feat)
        rows = jnp.concatenate([stack_six(feat, LEFT), jnp.zeros((HALF - 48, TILE), F32)], axis=0)
        left_ref[t * TILE : (t + 1) * TILE, :] = rows.T[:, :48].astype(BF16)


def prepare(targets, sources):
    return pl.pallas_call(
        prepare_kernel,
        out_shape=(shaped(1536, 48, dtype=BF16), shaped(48, SRC, dtype=BF16), shaped(8, SRC)),
        in_specs=[VMEM, VMEM],
        out_specs=(VMEM, VMEM, VMEM),
        compiler_params=PARAMS,
        name="prepare",
    )(targets, sources)


def layer_kernel(place_ref, left_ref, right_ref, moment_ref, trace_ref, fraction_ref, out_ref, acc):
    brick, row = place_ref[0], place_ref[1]
    acc[...] = jnp.zeros_like(acc)

    def chunk(c, carry):
        at = pl.multiple_of(c * CHUNK, CHUNK)
        trace = jnp.concatenate(
            [trace_ref[pl.ds(2 * c, 1), :], trace_ref[pl.ds(2 * c + 1, 1), :]], axis=1
        )
        face = moment_ref[:, pl.ds(at, CHUNK)] * trace
        face = stack_six(face, RIGHT).astype(BF16)
        dist = right_ref[:, pl.ds(at, CHUNK)]
        for t in range(1536 // TILE):
            rows = slice(t * TILE, (t + 1) * TILE)
            left = left_ref[rows, :]
            total = acc[rows, :]
            for n in range(CHUNK // 256):
                lanes = slice(n * 256, (n + 1) * 256)
                d = jnp.dot(left, dist[:, lanes], preferred_element_type=F32)
                f = jnp.dot(left, face[:, lanes], preferred_element_type=F32)
                r = lax.rsqrt(d)
                term = (f * r) * (r * r)
                total = total + term[:, :HALF] + term[:, HALF:]
            acc[rows, :] = total
        return carry

    lax.fori_loop(0, SRC // CHUNK, chunk, 0)
    for t in range(1536 // TILE):
        turned = acc[t * TILE : (t + 1) * TILE, :].T
        total = jnp.sum(turned, axis=0, keepdims=True)
        out_ref[:, t * TILE : (t + 1) * TILE] = total * (1.0 / (4.0 * math.pi))
    at = pl.multiple_of(row * 384, 128)
    own = (fraction_ref[...] - 1.0) * trace_ref[pl.ds(brick, 1), :]
    out_ref[:, pl.ds(at, 384)] = out_ref[:, pl.ds(at, 384)] + own


def layer(place, left, right, moment, traces, fraction):
    return pl.pallas_call(
        layer_kernel,
        out_shape=shaped(1, 1536),
        in_specs=[SMEM] + [VMEM] * 5,
        out_specs=VMEM,
        scratch_shapes=[pltpu.VMEM((1536, HALF), F32)],
        compiler_params=PARAMS,
        name="layer",
    )(place, left, right, moment, traces, fraction)


def answer_kernel(place_ref, part_ref, got_ref, out_ref, wide, table):
    row = place_ref[1]
    total = jnp.sum(part_ref[...], axis=0, keepdims=True)
    wide[...] = jnp.zeros_like(wide)
    lane = lax.broadcasted_iota(jnp.int32, (256, HALF), 1)
    wide[:, 0 : 3 * CAP] = got_ref[...]
    got = wide[...]
    slot = got.astype(jnp.int32)
    upper, lower = slot >> 7, slot & 127
    value = jnp.zeros((256, HALF), F32)
    for h in range(1536 // HALF):
        entry = jnp.broadcast_to(total[:, h * HALF : (h + 1) * HALF], (256, HALF))
        found = jnp.take_along_axis(entry, lower, axis=1)
        value = jnp.where(upper == h, found, value)
    cell = pltpu.roll(got, HALF - CAP, 1)
    pair = jnp.where(lane < CAP, value, jnp.where(lane < 2 * CAP, cell, 0.0))
    lane80 = lax.broadcasted_iota(jnp.int32, (80, HALF), 1)
    dead = jnp.where((lane80 >= CAP) & (lane80 < 2 * CAP), -1.0, 0.0)
    for q in range(6):
        table[q] = dead
    for q in range(4):
        table[q + 1, 8:72, :] = pair[q * 64 : (q + 1) * 64]
    for t in range(3):
        acc = jnp.zeros((64, HALF), F32)
        for s in range(5):
            piece = table[row + t, 6 + s : 70 + s, :]
            if s > 0:
                piece = pltpu.roll(piece, 2 * CAP * s, 1)
            acc = acc + piece
        out_ref[:, t * HALF : (t + 1) * HALF] = acc


def answer(place, partial, got):
    return pl.pallas_call(
        answer_kernel,
        out_shape=shaped(64, 384),
        in_specs=[SMEM, VMEM, VMEM],
        out_specs=VMEM,
        scratch_shapes=[pltpu.VMEM((256, HALF), F32), pltpu.VMEM((6, 80, HALF), F32)],
        compiler_params=PARAMS,
        name="answer",
    )(place, partial, got)


def second_kernel(place_ref, got_ref, first_ref, out_ref, mask, buf):
    brick, row = place_ref[0], place_ref[1]
    cells_x, cells_y = place_ref[2], place_ref[3]
    buf[0] = jnp.zeros((XD, YE, CZ), F32)
    z_at = lax.broadcasted_iota(jnp.int32, (CZ, HALF), 0)
    for t in range(3):
        block = got_ref[:, t * HALF : (t + 1) * HALF]
        turned = jnp.concatenate([block, pltpu.roll(block, HALF - 6, 1)], axis=0).T
        rows, begin = ((16, 0), (40, 8), (16, 40))[t]
        for s in range(5):
            planes, first_plane = ((4, 0), (8, 4), (8, 12), (8, 20), (4, 28))[s]
            x_off = 4 if s == 0 else 0
            hots, highs, lows = [], [], []
            row_at = lax.broadcasted_iota(jnp.int32, (planes * rows, HALF), 0)
            for k in range(6):
                value = turned[24 * s + k : 24 * s + k + 1, :]
                cell = turned[24 * s + CAP + k : 24 * s + CAP + k + 1, :].astype(jnp.int32)
                x = (cell >> 13) - x_off
                y = (cell >> 8) & 31
                live = (cell >= 0) & (x >= 0) & (x < planes)
                if t == 0:
                    live = live & (y >= 20)
                    y = y - 20
                else:
                    y = y + 4
                    if t == 2:
                        live = live & (y < 16)
                at = jnp.where(live, x * rows + y, -1)
                value = jnp.where(jnp.abs(value) < TINY, TINY, value)
                high = value.astype(BF16).astype(F32)
                hit = z_at == (cell & 255)
                hots.append(jnp.where(row_at == at, 1.0, 0.0).astype(BF16))
                highs.append(jnp.where(hit, high, 0.0).astype(BF16))
                lows.append(jnp.where(hit, value - high, 0.0).astype(BF16))
            hot = jnp.concatenate(hots, axis=1)
            total = None
            for part in (highs, lows):
                term = lax.dot_general(
                    hot, jnp.concatenate(part, axis=1), (((1,), (1,)), ((), ())), preferred_element_type=F32
                )
                total = term if total is None else total + term
            target = buf.at[0, first_plane : first_plane + planes, begin : begin + rows, :]
            target[...] = target[...] + total.reshape(planes, rows, CZ)
    y_at = lax.broadcasted_iota(jnp.int32, (YE, CZ), 0) + (row * CY - YO)
    in_y = (y_at >= 0) & (y_at < cells_y)

    def begin_plane(x, carry):
        v = buf[0, x]
        at = brick * CX + x - YO
        in_x = jnp.where((at >= 0) & (at < cells_x), 1.0, 0.0).astype(F32)
        mask[x] = jnp.where(in_y & (v == 0.0), in_x, 0.0)
        buf[0, x] = jnp.where(jnp.abs(v) < 2.0 * TINY, 0.0, v)
        return carry

    lax.fori_loop(0, XD, begin_plane, 0)
    for k in range(1, SWEEPS + 1):
        weight = WEIGHTS[k - 1]
        src, dst = buf.at[(k - 1) % 2], buf.at[k % 2]

        def plane(x, carry, src=src, dst=dst, weight=weight):
            free = mask[x]
            for h, (v, around) in enumerate(neighbours(src, x)):
                lanes = slice(h * HALF, (h + 1) * HALF)
                dst[x, :, lanes] = v + free[:, lanes] * ((weight / 6.0) * around - weight * v)
            return carry

        lax.fori_loop(k, XD - k, plane, 0)
    for x in range(CX):
        out_ref[x] = first_ref[x] + buf[SWEEPS % 2, x + YO, YO : YO + CY, :]


def second_solve(place, got, first):
    return pl.pallas_call(
        second_kernel,
        out_shape=shaped(CX, CY, CZ),
        in_specs=[SMEM, VMEM, VMEM],
        out_specs=VMEM,
        scratch_shapes=[pltpu.VMEM((XD, YE, CZ), F32), pltpu.VMEM((2, XD, YE, CZ), F32)],
        compiler_params=PARAMS,
        name="second_solve",
    )(place, got, first)


def shifted(x, axis, step):
    count = lax.axis_size(axis)
    pairs = [(i, i + step) for i in range(count) if 0 <= i + step < count]
    return lax.ppermute(x, axis, pairs)


def local(
    magnet, node_position, node_moment, solid_fraction, request_cell, request_slot, request_count
):
    bricks, rows = lax.axis_size("brick"), lax.axis_size("row")
    brick, row = lax.axis_index("brick"), lax.axis_index("row")
    place = jnp.stack([brick, row, jnp.int32(bricks * CX), jnp.int32(rows * CY)]).astype(jnp.int32)
    cell, slot = request_cell[0, 0], request_slot[0, 0]
    live = jnp.arange(CAP)[None, :] < request_count[0, 0][:, None]
    zeros = jnp.zeros((bricks, CAP), F32)
    slot_f = jnp.where(live, slot, DEAD_SLOT).astype(F32)
    cell_f = jnp.where(live, cell, -1).astype(F32)
    base = jnp.concatenate([slot_f, zeros, cell_f], axis=1)
    cells = cell.T.reshape(2, 6, bricks).transpose(1, 0, 2).reshape(6, 2 * bricks)
    grouped = jnp.concatenate([node_position, node_moment], axis=0).reshape(6, bricks, rows, 384)
    sources = lax.dynamic_index_in_dim(grouped, row, 2, keepdims=False).reshape(6, bricks * 384)
    targets = lax.dynamic_slice_in_dim(node_position, brick * 1536, 1536, 1)
    fraction = lax.dynamic_slice_in_dim(solid_fraction, brick * 1536 + row * 384, 384, 0)[None]
    left, right, moment = prepare(targets, sources)

    own, low, high = own_source(magnet)
    l1, r1 = shifted(own, "brick", 1), shifted(own, "brick", -1)
    l2, r2 = shifted(high, "brick", 2), shifted(low, "brick", -2)
    sx, upper, lower = join_x(own, l1, r1, l2, r2)
    below, above = shifted(upper, "row", 1), shifted(lower, "row", -1)
    first, message = first_solve(place, sx, below, above, cells, base)
    message = message.reshape(rows * bricks, 3 * CAP)
    got = lax.all_to_all(message, ("row", "brick"), split_axis=0, concat_axis=0, tiled=True)
    quarter = place_quarter(place, got)
    traces = lax.all_to_all(quarter, "brick", split_axis=0, concat_axis=0, tiled=True)
    partial = layer(place, left, right, moment, traces, fraction)
    partials = lax.all_gather(partial, "row", axis=0, tiled=True)
    reply = answer(place, partials, got)
    returned = lax.all_to_all(reply, "brick", split_axis=0, concat_axis=0, tiled=True)
    potential = second_solve(place, returned, first)
    begin = HALF + 2 * 2 * CAP
    boundary = jnp.where(live, returned[:, begin : begin + CAP], 0.0)
    return potential, boundary[None, None]


def solution(mesh):
    placed = (
        P(None, "brick", "row", None),
        P(),
        P(),
        P(),
        P("brick", "row", None, None),
        P("brick", "row", None, None),
        P("brick", "row", None),
    )
    return jax.shard_map(
        local,
        mesh=mesh,
        in_specs=placed,
        out_specs=(P("brick", "row", None), P("brick", "row", None, None)),
        check_vma=False,
    )
```

```python
import functools
import math

import jax
import jax.numpy as jnp
from jax import lax
from jax.experimental import pallas as pl
from jax.experimental.pallas import tpu as pltpu
from jax.sharding import PartitionSpec as P

CX = 8
CY = 32
CZ = 256
SWEEPS = 12
CAP = 12
RELAX_LOW = 0.5
RELAX_HIGH = 2.0
SOFTENING = 0.5

YO = 12
YE = CY + 24
XS = CX + 22
XD = CX + 24
HALF = 128
RIM = CY + 2
PARAMS = pltpu.CompilerParams(vmem_limit_bytes=50 * 1024 * 1024)
DEAD_SLOT = 4096
TINY = 1e-30
F32 = jnp.float32
BF16 = jnp.bfloat16
VMEM = pl.BlockSpec(memory_space=pltpu.VMEM)
SMEM = pl.BlockSpec(memory_space=pltpu.SMEM)


def sweep_weights(total_steps):
    centre = 0.5 * (RELAX_HIGH + RELAX_LOW)
    radius = 0.5 * (RELAX_HIGH - RELAX_LOW)
    root_list = [
        1.0 / (centre + radius * math.cos(math.pi * (2 * order_index + 1) / (2 * total_steps)))
        for order_index in range(total_steps)
    ]
    ordered = []
    for order_index in range(total_steps // 2):
        ordered.append(root_list[order_index])
        ordered.append(root_list[total_steps - 1 - order_index])
    return ordered


WEIGHTS = sweep_weights(SWEEPS)


def shaped(*dims, dtype=F32):
    return jax.ShapeDtypeStruct(dims, dtype)


def split3(v):
    hi = v.astype(BF16).astype(F32)
    rest = v - hi
    mid = rest.astype(BF16).astype(F32)
    return hi, mid, rest - mid


def z_pair(left, right):
    lane = lax.broadcasted_iota(jnp.int32, left.shape, 1)
    left_dn = pltpu.roll(left, 1, 1)
    right_dn = pltpu.roll(right, 1, 1)
    left_up = pltpu.roll(left, HALF - 1, 1)
    right_up = pltpu.roll(right, HALF - 1, 1)
    first, last = lane == 0, lane == HALF - 1
    dn = (jnp.where(first, 0.0, left_dn), jnp.where(first, left_dn, right_dn))
    up = (jnp.where(last, right_up, left_up), jnp.where(last, 0.0, right_up))
    return dn, up


def source_kernel(m_ref, e_ref, flat_ref, low_ref, high_ref, pad):
    pad[...] = jnp.zeros_like(pad)
    for x in range(CX):
        pad[0, x + 1, 12:44, :] = m_ref[0, x]
        pad[1, x + 1, 12:44, :] = m_ref[1, x]
        pad[2, x + 1, 12:44, :] = m_ref[2, x]
    zeros = jnp.zeros((40, CZ), F32)
    for i in range(CX + 2):
        ahead = pad[0, i + 1, 8:48, :] if i + 1 <= CX else zeros
        behind = pad[0, i - 1, 8:48, :] if i >= 2 else zeros
        total = ahead - behind
        if 1 <= i <= CX:
            total = total + (pad[1, i, 9:49, :] - pad[1, i, 7:47, :])
            c = pad[2, i, 8:48, :]
            dn, up = z_pair(c[:, :HALF], c[:, HALF:])
            total = total + jnp.concatenate([up[0] - dn[0], up[1] - dn[1]], axis=1)
        total = -0.5 * total
        e_ref[i] = total
        rim = e_ref[i, 3:37, :]
        flat_ref[i * RIM : (i + 1) * RIM, :] = rim
        if i < 4:
            low_ref[i * RIM : (i + 1) * RIM, :] = rim
        j = i - (CX - 2)
        if j >= 0:
            high_ref[j * RIM : (j + 1) * RIM, :] = rim


def own_source(magnet):
    return pl.pallas_call(
        source_kernel,
        out_shape=(
            shaped(10, 40, CZ),
            shaped(10 * RIM, CZ),
            shaped(4 * RIM, CZ),
            shaped(4 * RIM, CZ),
        ),
        in_specs=[VMEM],
        out_specs=(VMEM,) * 4,
        scratch_shapes=[pltpu.VMEM((3, CX + 2, 56, CZ), F32)],
        compiler_params=PARAMS,
        name="own_source",
    )(magnet)


def beside(plane, before, own):
    return max(before - plane, plane - (before + own - 1), 0)


def y_rows():
    counts = [CX + 4 - beside(plane, 11, CX) for plane in range(XS)]
    begins = [sum(counts[:plane]) for plane in range(XS)]
    return counts, begins, -(-sum(counts) // 8) * 8


Y_COUNTS, Y_BEGINS, Y_TOTAL = y_rows()


def join_kernel(e_ref, l1_ref, r1_ref, l2_ref, r2_ref, sx_ref, upper_ref, lower_ref):
    parts = ((l1_ref, 2, 10), (r1_ref, 18, 10), (l2_ref, 0, 4), (r2_ref, 26, 4))
    upper_ref[Y_TOTAL - 8 :, :] = jnp.zeros((8, CZ), F32)
    lower_ref[Y_TOTAL - 8 :, :] = jnp.zeros((8, CZ), F32)
    for plane in range(XS):
        own = 10 <= plane < 20
        sx_ref[plane] = e_ref[plane - 10] if own else jnp.zeros((40, CZ), F32)
        total = sx_ref[plane, 3:37, :] if own else None
        for ref, begin, count in parts:
            if begin <= plane < begin + count:
                at = (plane - begin) * RIM
                term = ref[at : at + RIM, :]
                total = term if total is None else total + term
        sx_ref[plane, 3:37, :] = total
        rows, at = Y_COUNTS[plane], Y_BEGINS[plane]
        upper_ref[at : at + rows, :] = sx_ref[plane, 37 - rows : 37, :]
        lower_ref[at : at + rows, :] = sx_ref[plane, 3 : 3 + rows, :]


def join_x(own, l1, r1, l2, r2):
    return pl.pallas_call(
        join_kernel,
        out_shape=(shaped(XS, 40, CZ), shaped(Y_TOTAL, CZ), shaped(Y_TOTAL, CZ)),
        in_specs=[VMEM] * 5,
        out_specs=(VMEM,) * 3,
        compiler_params=PARAMS,
        name="join_x",
    )(own, l1, r1, l2, r2)


def plane_rows(reach):
    return (0, YE) if reach > 3 else (8, YE - 8)


def neighbours(src, x, rows):
    begin, end = rows
    c = src[x, begin:end, :]
    around_x = src[x - 1, begin:end, :] + src[x + 1, begin:end, :]
    halves = (c[:, :HALF], c[:, HALF:])
    dn, up = z_pair(*halves)
    out = []
    for h in range(2):
        v = halves[h]
        around_y = pltpu.roll(v, 1, 0) + pltpu.roll(v, end - begin - 1, 0)
        around = around_x[:, h * HALF : (h + 1) * HALF] + around_y + (dn[h] + up[h])
        out.append((v, around))
    return out


def first_kernel(place_ref, sx_ref, below_ref, above_ref, cell_ref, base_ref, field_ref, msg_ref, s, buf):
    brick, row = place_ref[0], place_ref[1]
    cells_x, cells_y = place_ref[2], place_ref[3]
    y_at = lax.broadcasted_iota(jnp.int32, (YE, HALF), 0) + (row * CY - YO)
    in_y = jnp.where((y_at >= 0) & (y_at < cells_y), 1.0, 0.0).astype(F32)

    def x_scale(x, scale):
        at = brick * CX + x - 11
        return jnp.where((at >= 0) & (at < cells_x), scale, 0.0).astype(F32)

    edge = jnp.zeros((8, CZ), F32)
    for x in range(XS):
        s[x, 0:8, :] = edge
        s[x, 48:56, :] = edge
        s[x, 8:48, :] = sx_ref[x]
        rows, at = Y_COUNTS[x], Y_BEGINS[x]
        s[x, 13 - rows : 13, :] += below_ref[at : at + rows, :]
        s[x, 43 : 43 + rows, :] += above_ref[at : at + rows, :]
        coef = in_y * x_scale(x, WEIGHTS[0] / 6.0)
        full = s[x]
        buf[0, x, :, :HALF] = coef * full[:, :HALF]
        buf[0, x, :, HALF:] = coef * full[:, HALF:]
    for k in range(1, SWEEPS):
        weight = WEIGHTS[k]
        src, dst = buf.at[(k - 1) % 2], buf.at[k % 2]

        for x in range(k, XS - k):
            rows = plane_rows(SWEEPS - 1 - k - beside(x, 11, CX))
            begin, end = rows
            coef = in_y[begin:end] * x_scale(x, weight / 6.0)
            source = s[x, begin:end, :]
            for h, (v, around) in enumerate(neighbours(src, x, rows)):
                lanes = slice(h * HALF, (h + 1) * HALF)
                dst[x, begin:end, lanes] = (1.0 - weight) * v + coef * (source[:, lanes] + around)
    last = (SWEEPS - 1) % 2
    for x in range(CX):
        field_ref[x] = buf[last, x + 11, YO : YO + CY, :]
    flat = field_ref[...].reshape(CX * CY, CZ)
    turned = flat.T
    parts = [p.astype(BF16) for p in split3(turned)]
    row_at = lax.broadcasted_iota(jnp.int32, (CX * CY, HALF), 0)
    picked = []
    for k in range(6):
        cell = cell_ref[k : k + 1, :]
        hot = jnp.where(row_at == (cell >> 8), 1.0, 0.0).astype(BF16)
        at_rows = sum(jnp.dot(p, hot, preferred_element_type=F32) for p in parts)
        kept = jnp.where(row_at == (cell & 255), at_rows, 0.0)
        picked.append(jnp.sum(kept, axis=0, keepdims=True))
    sub = lax.broadcasted_iota(jnp.int32, (HALF, HALF), 0)
    tile = jnp.zeros((HALF, HALF), F32)
    for k in range(6):
        tile = jnp.where(sub == k, picked[k], tile)
    turned_tile = tile.T
    both = turned_tile[0:64] + pltpu.roll(turned_tile[64:128], 6, 1)
    traces = pltpu.roll(both, CAP, 1)
    lanes = 3 * CAP
    full = base_ref[...] + traces[:, :lanes]
    for q in range(4):
        msg_ref[q] = full


def first_solve(place, sx, below, above, cells, base):
    return pl.pallas_call(
        first_kernel,
        out_shape=(shaped(CX, CY, CZ), shaped(4, 64, 3 * CAP)),
        in_specs=[SMEM] + [VMEM] * 5,
        out_specs=(VMEM, VMEM),
        scratch_shapes=[pltpu.VMEM((XS, YE, CZ), F32), pltpu.VMEM((2, XS, YE, CZ), F32)],
        compiler_params=PARAMS,
        name="first_solve",
    )(place, sx, below, above, cells, base)


def place_kernel(place_ref, got_ref, out_ref):
    row = place_ref[1]
    got = got_ref[...]
    at = (lax.broadcasted_iota(jnp.int32, (256, 384), 1) + row * 384).astype(F32)
    acc = jnp.zeros((256, 384), F32)
    for i in range(CAP):
        slot = got[:, i : i + 1]
        trace = got[:, CAP + i : CAP + i + 1]
        acc = acc + jnp.where(at == slot, trace, 0.0)
    total = jnp.sum(acc, axis=0, keepdims=True)
    out_ref[...] = jnp.broadcast_to(total, (64, 384))


def place_quarter(place, got):
    return pl.pallas_call(
        place_kernel,
        out_shape=shaped(64, 384),
        in_specs=[SMEM, VMEM],
        out_specs=VMEM,
        compiler_params=PARAMS,
        name="place_quarter",
    )(place, got)


SRC = 24576
BLOCK = 1536
QUARTER = 384
CHUNK = 768
TILE = 128


def stack_six(v, order):
    parts = split3(v)
    return jnp.concatenate([parts[i] for i in order], axis=0)


RIGHT = (0, 1, 2, 0, 1, 0)
LEFT = (0, 0, 0, 1, 1, 2)


def prepare_kernel(place_ref, position_ref, moment_ref, left_ref, right_ref, face_ref):
    brick, row = place_ref[0], place_ref[1]
    sub = lax.broadcasted_iota(jnp.int32, (8, QUARTER), 0)

    def sources(b, carry):
        node = pl.multiple_of(b * BLOCK + row * QUARTER, HALF)
        at = pl.multiple_of(b * QUARTER, HALF)
        pos = position_ref[:, pl.ds(node, QUARTER)] - 4.0
        mom = moment_ref[:, pl.ds(node, QUARTER)]
        norm = jnp.sum(pos * pos, axis=0, keepdims=True)
        across = jnp.sum(pos * mom, axis=0, keepdims=True)
        dist = jnp.where(sub == 3, 1.0, jnp.where(sub == 4, norm, 0.0))
        face = jnp.where(sub == 4, -across, 0.0)
        for i in range(3):
            dist = jnp.where(sub == i, -2.0 * pos[i : i + 1], dist)
            face = jnp.where(sub == i, mom[i : i + 1], face)
        right_ref[:, pl.ds(at, QUARTER)] = stack_six(dist, RIGHT).astype(BF16)
        face_ref[:, pl.ds(at, QUARTER)] = face
        return carry

    lax.fori_loop(0, SRC // QUARTER, sources, 0, unroll=2)
    sub = lax.broadcasted_iota(jnp.int32, (8, TILE), 0)
    for t in range(BLOCK // TILE):
        node = pl.multiple_of(brick * BLOCK + t * TILE, HALF)
        pos = position_ref[:, pl.ds(node, TILE)] - 4.0
        norm = jnp.sum(pos * pos, axis=0, keepdims=True) + SOFTENING
        feat = jnp.where(sub == 3, norm, jnp.where(sub == 4, 1.0, 0.0))
        for i in range(3):
            feat = jnp.where(sub == i, pos[i : i + 1], feat)
        rows = jnp.concatenate([stack_six(feat, LEFT), jnp.zeros((HALF - 48, TILE), F32)], axis=0)
        left_ref[t * TILE : (t + 1) * TILE, :] = rows.T[:, :48].astype(BF16)


def prepare(place, position, moment):
    return pl.pallas_call(
        prepare_kernel,
        out_shape=(shaped(BLOCK, 48, dtype=BF16), shaped(48, SRC, dtype=BF16), shaped(8, SRC)),
        in_specs=[SMEM, VMEM, VMEM],
        out_specs=(VMEM, VMEM, VMEM),
        compiler_params=PARAMS,
        name="prepare",
    )(place, position, moment)


def layer_kernel(place_ref, left_ref, right_ref, moment_ref, trace_ref, fraction_ref, out_ref, acc):
    brick, row = place_ref[0], place_ref[1]
    acc[...] = jnp.zeros_like(acc)

    def chunk(c, carry):
        at = pl.multiple_of(c * CHUNK, CHUNK)
        trace = jnp.concatenate(
            [trace_ref[pl.ds(2 * c, 1), :], trace_ref[pl.ds(2 * c + 1, 1), :]], axis=1
        )
        face = moment_ref[:, pl.ds(at, CHUNK)] * trace
        face = stack_six(face, RIGHT).astype(BF16)
        dist = right_ref[:, pl.ds(at, CHUNK)]
        for t in range(1536 // TILE):
            rows = slice(t * TILE, (t + 1) * TILE)
            left = left_ref[rows, :]
            total = acc[rows, :]
            for n in range(CHUNK // 256):
                lanes = slice(n * 256, (n + 1) * 256)
                d = jnp.dot(left, dist[:, lanes], preferred_element_type=F32)
                f = jnp.dot(left, face[:, lanes], preferred_element_type=F32)
                r = lax.rsqrt(d)
                term = (f * r) * (r * r)
                total = total + term[:, :HALF] + term[:, HALF:]
            acc[rows, :] = total
        return carry

    lax.fori_loop(0, SRC // CHUNK, chunk, 0)
    for t in range(1536 // TILE):
        turned = acc[t * TILE : (t + 1) * TILE, :].T
        total = jnp.sum(turned, axis=0, keepdims=True)
        out_ref[:, t * TILE : (t + 1) * TILE] = total * (1.0 / (4.0 * math.pi))
    at = pl.multiple_of(row * 384, 128)
    own = (fraction_ref[...] - 1.0) * trace_ref[pl.ds(brick, 1), :]
    out_ref[:, pl.ds(at, 384)] = out_ref[:, pl.ds(at, 384)] + own


def layer(place, left, right, moment, traces, fraction):
    return pl.pallas_call(
        layer_kernel,
        out_shape=shaped(1, 1536),
        in_specs=[SMEM] + [VMEM] * 5,
        out_specs=VMEM,
        scratch_shapes=[pltpu.VMEM((1536, HALF), F32)],
        compiler_params=PARAMS,
        name="layer",
    )(place, left, right, moment, traces, fraction)


def answer_kernel(place_ref, part_ref, got_ref, out_ref, wide, table):
    row = place_ref[1]
    total = jnp.sum(part_ref[...], axis=0, keepdims=True)
    wide[...] = jnp.zeros_like(wide)
    lane = lax.broadcasted_iota(jnp.int32, (256, HALF), 1)
    wide[:, 0 : 3 * CAP] = got_ref[...]
    got = wide[...]
    slot = got.astype(jnp.int32)
    upper, lower = slot >> 7, slot & 127
    value = jnp.zeros((256, HALF), F32)
    for h in range(1536 // HALF):
        entry = jnp.broadcast_to(total[:, h * HALF : (h + 1) * HALF], (256, HALF))
        found = jnp.take_along_axis(entry, lower, axis=1)
        value = jnp.where(upper == h, found, value)
    cell = pltpu.roll(got, HALF - CAP, 1)
    pair = jnp.where(lane < CAP, value, jnp.where(lane < 2 * CAP, cell, 0.0))
    lane80 = lax.broadcasted_iota(jnp.int32, (80, HALF), 1)
    dead = jnp.where((lane80 >= CAP) & (lane80 < 2 * CAP), -1.0, 0.0)
    for q in range(6):
        table[q] = dead
    for q in range(4):
        table[q + 1, 8:72, :] = pair[q * 64 : (q + 1) * 64]
    for t in range(3):
        acc = jnp.zeros((64, HALF), F32)
        for s in range(5):
            piece = table[row + t, 6 + s : 70 + s, :]
            if s > 0:
                piece = pltpu.roll(piece, 2 * CAP * s, 1)
            acc = acc + piece
        out_ref[:, t * HALF : (t + 1) * HALF] = acc


def answer(place, partial, got):
    return pl.pallas_call(
        answer_kernel,
        out_shape=shaped(64, 384),
        in_specs=[SMEM, VMEM, VMEM],
        out_specs=VMEM,
        scratch_shapes=[pltpu.VMEM((256, HALF), F32), pltpu.VMEM((6, 80, HALF), F32)],
        compiler_params=PARAMS,
        name="answer",
    )(place, partial, got)


def second_kernel(place_ref, got_ref, first_ref, out_ref, mask, buf):
    brick, row = place_ref[0], place_ref[1]
    cells_x, cells_y = place_ref[2], place_ref[3]
    buf[0] = jnp.zeros((XD, YE, CZ), F32)
    z_at = lax.broadcasted_iota(jnp.int32, (CZ, HALF), 0)
    for t in range(3):
        block = got_ref[:, t * HALF : (t + 1) * HALF]
        turned = jnp.concatenate([block, pltpu.roll(block, HALF - 6, 1)], axis=0).T
        rows, begin = ((16, 0), (40, 8), (16, 40))[t]
        for s in range(5):
            planes, first_plane = ((4, 0), (8, 4), (8, 12), (8, 20), (4, 28))[s]
            x_off = 4 if s == 0 else 0
            hots, highs, lows = [], [], []
            row_at = lax.broadcasted_iota(jnp.int32, (planes * rows, HALF), 0)
            for k in range(6):
                value = turned[24 * s + k : 24 * s + k + 1, :]
                cell = turned[24 * s + CAP + k : 24 * s + CAP + k + 1, :].astype(jnp.int32)
                x = (cell >> 13) - x_off
                y = (cell >> 8) & 31
                live = (cell >= 0) & (x >= 0) & (x < planes)
                if t == 0:
                    live = live & (y >= 20)
                    y = y - 20
                else:
                    y = y + 4
                    if t == 2:
                        live = live & (y < 16)
                at = jnp.where(live, x * rows + y, -1)
                value = jnp.where(jnp.abs(value) < TINY, TINY, value)
                high = value.astype(BF16).astype(F32)
                hit = z_at == (cell & 255)
                hots.append(jnp.where(row_at == at, 1.0, 0.0).astype(BF16))
                highs.append(jnp.where(hit, high, 0.0).astype(BF16))
                lows.append(jnp.where(hit, value - high, 0.0).astype(BF16))
            hot = jnp.concatenate(hots, axis=1)
            total = None
            for part in (highs, lows):
                term = lax.dot_general(
                    hot, jnp.concatenate(part, axis=1), (((1,), (1,)), ((), ())), preferred_element_type=F32
                )
                total = term if total is None else total + term
            target = buf.at[0, first_plane : first_plane + planes, begin : begin + rows, :]
            target[...] = target[...] + total.reshape(planes, rows, CZ)
    y_at = lax.broadcasted_iota(jnp.int32, (YE, CZ), 0) + (row * CY - YO)
    in_y = (y_at >= 0) & (y_at < cells_y)

    def begin_plane(x, carry):
        v = buf[0, x]
        at = brick * CX + x - YO
        in_x = jnp.where((at >= 0) & (at < cells_x), 1.0, 0.0).astype(F32)
        mask[x] = jnp.where(in_y & (v == 0.0), in_x, 0.0)
        buf[0, x] = jnp.where(jnp.abs(v) < 2.0 * TINY, 0.0, v)
        return carry

    lax.fori_loop(0, XD, begin_plane, 0)
    for k in range(1, SWEEPS + 1):
        weight = WEIGHTS[k - 1]
        src, dst = buf.at[(k - 1) % 2], buf.at[k % 2]

        for x in range(k, XD - k):
            rows = plane_rows(SWEEPS - k - beside(x, YO, CX))
            begin, end = rows
            free = mask[x, begin:end, :]
            for h, (v, around) in enumerate(neighbours(src, x, rows)):
                lanes = slice(h * HALF, (h + 1) * HALF)
                dst[x, begin:end, lanes] = v + free[:, lanes] * ((weight / 6.0) * around - weight * v)
    for x in range(CX):
        out_ref[x] = first_ref[x] + buf[SWEEPS % 2, x + YO, YO : YO + CY, :]


def second_solve(place, got, first):
    return pl.pallas_call(
        second_kernel,
        out_shape=shaped(CX, CY, CZ),
        in_specs=[SMEM, VMEM, VMEM],
        out_specs=VMEM,
        scratch_shapes=[pltpu.VMEM((XD, YE, CZ), F32), pltpu.VMEM((2, XD, YE, CZ), F32)],
        compiler_params=PARAMS,
        name="second_solve",
    )(place, got, first)


def shifted(x, axis, step):
    count = lax.axis_size(axis)
    pairs = [(i, i + step) for i in range(count) if 0 <= i + step < count]
    return lax.ppermute(x, axis, pairs)


def local(
    magnet, node_position, node_moment, solid_fraction, request_cell, request_slot, request_count
):
    bricks, rows = lax.axis_size("brick"), lax.axis_size("row")
    brick, row = lax.axis_index("brick"), lax.axis_index("row")
    place = jnp.stack([brick, row, jnp.int32(bricks * CX), jnp.int32(rows * CY)]).astype(jnp.int32)
    cell, slot = request_cell[0, 0], request_slot[0, 0]
    live = jnp.arange(CAP)[None, :] < request_count[0, 0][:, None]
    zeros = jnp.zeros((bricks, CAP), F32)
    slot_f = jnp.where(live, slot, DEAD_SLOT).astype(F32)
    cell_f = jnp.where(live, cell, -1).astype(F32)
    base = jnp.concatenate([slot_f, zeros, cell_f], axis=1)
    cells = cell.T.reshape(2, 6, bricks).transpose(1, 0, 2).reshape(6, 2 * bricks)
    fraction = lax.dynamic_slice_in_dim(solid_fraction, brick * 1536 + row * 384, 384, 0)[None]
    left, right, moment = prepare(place, node_position, node_moment)

    own, flat, low, high = own_source(magnet)
    l1, r1 = shifted(flat, "brick", 1), shifted(flat, "brick", -1)
    l2, r2 = shifted(high, "brick", 2), shifted(low, "brick", -2)
    sx, upper, lower = join_x(own, l1, r1, l2, r2)
    below, above = shifted(upper, "row", 1), shifted(lower, "row", -1)
    first, message = first_solve(place, sx, below, above, cells, base)
    message = message.reshape(rows * bricks, 3 * CAP)
    got = lax.all_to_all(message, ("row", "brick"), split_axis=0, concat_axis=0, tiled=True)
    quarter = place_quarter(place, got)
    traces = lax.all_to_all(quarter, "brick", split_axis=0, concat_axis=0, tiled=True)
    partial = layer(place, left, right, moment, traces, fraction)
    partials = lax.all_gather(partial, "row", axis=0, tiled=True)
    reply = answer(place, partials, got)
    returned = lax.all_to_all(reply, "brick", split_axis=0, concat_axis=0, tiled=True)
    potential = second_solve(place, returned, first)
    begin = HALF + 2 * 2 * CAP
    boundary = jnp.where(live, returned[:, begin : begin + CAP], 0.0)
    return potential, boundary[None, None]


def solution(mesh):
    placed = (
        P(None, "brick", "row", None),
        P(),
        P(),
        P(),
        P("brick", "row", None, None),
        P("brick", "row", None, None),
        P("brick", "row", None),
    )
    return jax.shard_map(
        local,
        mesh=mesh,
        in_specs=placed,
        out_specs=(P("brick", "row", None), P("brick", "row", None, None)),
        check_vma=False,
    )
```

```python
import functools
import math

import jax
import jax.numpy as jnp
from jax import lax
from jax.experimental import pallas as pl
from jax.experimental.pallas import tpu as pltpu
from jax.sharding import PartitionSpec as P

CX = 8
CY = 32
CZ = 256
SWEEPS = 12
CAP = 12
RELAX_LOW = 0.5
RELAX_HIGH = 2.0
SOFTENING = 0.5

YO = 12
YE = CY + 24
XS = CX + 22
XD = CX + 24
HALF = 128
RIM = CY + 2
PARAMS = pltpu.CompilerParams(vmem_limit_bytes=50 * 1024 * 1024)
DEAD_SLOT = 4096
TINY = 1e-30
F32 = jnp.float32
BF16 = jnp.bfloat16
VMEM = pl.BlockSpec(memory_space=pltpu.VMEM)
SMEM = pl.BlockSpec(memory_space=pltpu.SMEM)


def sweep_weights(total_steps):
    centre = 0.5 * (RELAX_HIGH + RELAX_LOW)
    radius = 0.5 * (RELAX_HIGH - RELAX_LOW)
    root_list = [
        1.0 / (centre + radius * math.cos(math.pi * (2 * order_index + 1) / (2 * total_steps)))
        for order_index in range(total_steps)
    ]
    ordered = []
    for order_index in range(total_steps // 2):
        ordered.append(root_list[order_index])
        ordered.append(root_list[total_steps - 1 - order_index])
    return ordered


WEIGHTS = sweep_weights(SWEEPS)


def shaped(*dims, dtype=F32):
    return jax.ShapeDtypeStruct(dims, dtype)


def split3(v):
    hi = v.astype(BF16).astype(F32)
    rest = v - hi
    mid = rest.astype(BF16).astype(F32)
    return hi, mid, rest - mid


def z_pair(left, right):
    lane = lax.broadcasted_iota(jnp.int32, left.shape, 1)
    left_dn = pltpu.roll(left, 1, 1)
    right_dn = pltpu.roll(right, 1, 1)
    left_up = pltpu.roll(left, HALF - 1, 1)
    right_up = pltpu.roll(right, HALF - 1, 1)
    first, last = lane == 0, lane == HALF - 1
    dn = (jnp.where(first, 0.0, left_dn), jnp.where(first, left_dn, right_dn))
    up = (jnp.where(last, right_up, left_up), jnp.where(last, 0.0, right_up))
    return dn, up


def source_kernel(m_ref, e_ref, flat_ref, low_ref, high_ref, pad):
    pad[...] = jnp.zeros_like(pad)
    for x in range(CX):
        pad[0, x + 1, 12:44, :] = m_ref[0, x]
        pad[1, x + 1, 12:44, :] = m_ref[1, x]
        pad[2, x + 1, 12:44, :] = m_ref[2, x]
    zeros = jnp.zeros((40, CZ), F32)
    for i in range(CX + 2):
        ahead = pad[0, i + 1, 8:48, :] if i + 1 <= CX else zeros
        behind = pad[0, i - 1, 8:48, :] if i >= 2 else zeros
        total = ahead - behind
        if 1 <= i <= CX:
            total = total + (pad[1, i, 9:49, :] - pad[1, i, 7:47, :])
            c = pad[2, i, 8:48, :]
            dn, up = z_pair(c[:, :HALF], c[:, HALF:])
            total = total + jnp.concatenate([up[0] - dn[0], up[1] - dn[1]], axis=1)
        total = -0.5 * total
        e_ref[i] = total
        rim = e_ref[i, 3:37, :]
        flat_ref[i * RIM : (i + 1) * RIM, :] = rim
        if i < 4:
            low_ref[i * RIM : (i + 1) * RIM, :] = rim
        j = i - (CX - 2)
        if j >= 0:
            high_ref[j * RIM : (j + 1) * RIM, :] = rim


def own_source(magnet):
    return pl.pallas_call(
        source_kernel,
        out_shape=(
            shaped(10, 40, CZ),
            shaped(10 * RIM, CZ),
            shaped(4 * RIM, CZ),
            shaped(4 * RIM, CZ),
        ),
        in_specs=[VMEM],
        out_specs=(VMEM,) * 4,
        scratch_shapes=[pltpu.VMEM((3, CX + 2, 56, CZ), F32)],
        compiler_params=PARAMS,
        name="own_source",
    )(magnet)


def beside(plane, before, own):
    return max(before - plane, plane - (before + own - 1), 0)


def y_rows():
    counts = [CX + 4 - beside(plane, 11, CX) for plane in range(XS)]
    begins = [sum(counts[:plane]) for plane in range(XS)]
    return counts, begins, -(-sum(counts) // 8) * 8


Y_COUNTS, Y_BEGINS, Y_TOTAL = y_rows()


def join_kernel(e_ref, l1_ref, r1_ref, l2_ref, r2_ref, order_ref, sx_ref, upper_ref, lower_ref):
    del order_ref
    parts = ((l1_ref, 2, 10), (r1_ref, 18, 10), (l2_ref, 0, 4), (r2_ref, 26, 4))
    upper_ref[Y_TOTAL - 8 :, :] = jnp.zeros((8, CZ), F32)
    lower_ref[Y_TOTAL - 8 :, :] = jnp.zeros((8, CZ), F32)
    for plane in range(XS):
        own = 10 <= plane < 20
        sx_ref[plane] = e_ref[plane - 10] if own else jnp.zeros((40, CZ), F32)
        total = sx_ref[plane, 3:37, :] if own else None
        for ref, begin, count in parts:
            if begin <= plane < begin + count:
                at = (plane - begin) * RIM
                term = ref[at : at + RIM, :]
                total = term if total is None else total + term
        sx_ref[plane, 3:37, :] = total
        rows, at = Y_COUNTS[plane], Y_BEGINS[plane]
        upper_ref[at : at + rows, :] = sx_ref[plane, 37 - rows : 37, :]
        lower_ref[at : at + rows, :] = sx_ref[plane, 3 : 3 + rows, :]


def join_x(own, l1, r1, l2, r2, order):
    return pl.pallas_call(
        join_kernel,
        out_shape=(shaped(XS, 40, CZ), shaped(Y_TOTAL, CZ), shaped(Y_TOTAL, CZ)),
        in_specs=[VMEM] * 6,
        out_specs=(VMEM,) * 3,
        compiler_params=PARAMS,
        name="join_x",
    )(own, l1, r1, l2, r2, order)


def plane_rows(reach):
    return (0, YE) if reach > 3 else (8, YE - 8)


def neighbours(src, x, rows):
    begin, end = rows
    c = src[x, begin:end, :]
    around_x = src[x - 1, begin:end, :] + src[x + 1, begin:end, :]
    halves = (c[:, :HALF], c[:, HALF:])
    dn, up = z_pair(*halves)
    out = []
    for h in range(2):
        v = halves[h]
        around_y = pltpu.roll(v, 1, 0) + pltpu.roll(v, end - begin - 1, 0)
        around = around_x[:, h * HALF : (h + 1) * HALF] + around_y + (dn[h] + up[h])
        out.append((v, around))
    return out


def first_kernel(place_ref, sx_ref, below_ref, above_ref, cell_ref, base_ref, field_ref, msg_ref, s, buf):
    brick, row = place_ref[0], place_ref[1]
    cells_x, cells_y = place_ref[2], place_ref[3]
    y_at = lax.broadcasted_iota(jnp.int32, (YE, HALF), 0) + (row * CY - YO)
    in_y = jnp.where((y_at >= 0) & (y_at < cells_y), 1.0, 0.0).astype(F32)

    def x_scale(x, scale):
        at = brick * CX + x - 11
        return jnp.where((at >= 0) & (at < cells_x), scale, 0.0).astype(F32)

    edge = jnp.zeros((8, CZ), F32)
    for x in range(XS):
        s[x, 0:8, :] = edge
        s[x, 48:56, :] = edge
        s[x, 8:48, :] = sx_ref[x]
        rows, at = Y_COUNTS[x], Y_BEGINS[x]
        s[x, 13 - rows : 13, :] += below_ref[at : at + rows, :]
        s[x, 43 : 43 + rows, :] += above_ref[at : at + rows, :]
        coef = in_y * x_scale(x, WEIGHTS[0] / 6.0)
        full = s[x]
        buf[0, x, :, :HALF] = coef * full[:, :HALF]
        buf[0, x, :, HALF:] = coef * full[:, HALF:]
    for k in range(1, SWEEPS):
        weight = WEIGHTS[k]
        src, dst = buf.at[(k - 1) % 2], buf.at[k % 2]

        for x in range(k, XS - k):
            rows = plane_rows(SWEEPS - 1 - k - beside(x, 11, CX))
            begin, end = rows
            coef = in_y[begin:end] * x_scale(x, weight / 6.0)
            source = s[x, begin:end, :]
            for h, (v, around) in enumerate(neighbours(src, x, rows)):
                lanes = slice(h * HALF, (h + 1) * HALF)
                dst[x, begin:end, lanes] = (1.0 - weight) * v + coef * (source[:, lanes] + around)
    last = (SWEEPS - 1) % 2
    for x in range(CX):
        field_ref[x] = buf[last, x + 11, YO : YO + CY, :]
    flat = field_ref[...].reshape(CX * CY, CZ)
    turned = flat.T
    parts = [p.astype(BF16) for p in split3(turned)]
    row_at = lax.broadcasted_iota(jnp.int32, (CX * CY, HALF), 0)
    picked = []
    for k in range(6):
        cell = cell_ref[k : k + 1, :]
        hot = jnp.where(row_at == (cell >> 8), 1.0, 0.0).astype(BF16)
        at_rows = sum(jnp.dot(p, hot, preferred_element_type=F32) for p in parts)
        kept = jnp.where(row_at == (cell & 255), at_rows, 0.0)
        picked.append(jnp.sum(kept, axis=0, keepdims=True))
    sub = lax.broadcasted_iota(jnp.int32, (HALF, HALF), 0)
    tile = jnp.zeros((HALF, HALF), F32)
    for k in range(6):
        tile = jnp.where(sub == k, picked[k], tile)
    turned_tile = tile.T
    both = turned_tile[0:64] + pltpu.roll(turned_tile[64:128], 6, 1)
    traces = pltpu.roll(both, CAP, 1)
    lanes = 3 * CAP
    full = base_ref[...] + traces[:, :lanes]
    for q in range(4):
        msg_ref[q] = full


def first_solve(place, sx, below, above, cells, base):
    return pl.pallas_call(
        first_kernel,
        out_shape=(shaped(CX, CY, CZ), shaped(4, 64, 3 * CAP)),
        in_specs=[SMEM] + [VMEM] * 5,
        out_specs=(VMEM, VMEM),
        scratch_shapes=[pltpu.VMEM((XS, YE, CZ), F32), pltpu.VMEM((2, XS, YE, CZ), F32)],
        compiler_params=PARAMS,
        name="first_solve",
    )(place, sx, below, above, cells, base)


def place_kernel(place_ref, got_ref, out_ref):
    row = place_ref[1]
    got = got_ref[...]
    at = (lax.broadcasted_iota(jnp.int32, (256, 384), 1) + row * 384).astype(F32)
    acc = jnp.zeros((256, 384), F32)
    for i in range(CAP):
        slot = got[:, i : i + 1]
        trace = got[:, CAP + i : CAP + i + 1]
        acc = acc + jnp.where(at == slot, trace, 0.0)
    total = jnp.sum(acc, axis=0, keepdims=True)
    out_ref[...] = jnp.broadcast_to(total, (64, 384))


def place_quarter(place, got):
    return pl.pallas_call(
        place_kernel,
        out_shape=shaped(64, 384),
        in_specs=[SMEM, VMEM],
        out_specs=VMEM,
        compiler_params=PARAMS,
        name="place_quarter",
    )(place, got)


SRC = 24576
BLOCK = 1536
QUARTER = 384
CHUNK = 768
TILE = 128


def stack_six(v, order):
    parts = split3(v)
    return jnp.concatenate([parts[i] for i in order], axis=0)


RIGHT = (0, 1, 2, 0, 1, 0)
LEFT = (0, 0, 0, 1, 1, 2)


def prepare_kernel(place_ref, position_ref, moment_ref, left_ref, right_ref, face_ref, order_ref):
    brick, row = place_ref[0], place_ref[1]
    sub = lax.broadcasted_iota(jnp.int32, (8, QUARTER), 0)
    order_ref[...] = jnp.zeros((8, HALF), F32)

    def sources(b, carry):
        node = pl.multiple_of(b * BLOCK + row * QUARTER, HALF)
        at = pl.multiple_of(b * QUARTER, HALF)
        pos = position_ref[:, pl.ds(node, QUARTER)] - 4.0
        mom = moment_ref[:, pl.ds(node, QUARTER)]
        norm = jnp.sum(pos * pos, axis=0, keepdims=True)
        across = jnp.sum(pos * mom, axis=0, keepdims=True)
        dist = jnp.where(sub == 3, 1.0, jnp.where(sub == 4, norm, 0.0))
        face = jnp.where(sub == 4, -across, 0.0)
        for i in range(3):
            dist = jnp.where(sub == i, -2.0 * pos[i : i + 1], dist)
            face = jnp.where(sub == i, mom[i : i + 1], face)
        right_ref[:, pl.ds(at, QUARTER)] = stack_six(dist, RIGHT).astype(BF16)
        face_ref[:, pl.ds(at, QUARTER)] = face
        return carry

    lax.fori_loop(0, SRC // QUARTER, sources, 0, unroll=2)
    sub = lax.broadcasted_iota(jnp.int32, (8, TILE), 0)
    for t in range(BLOCK // TILE):
        node = pl.multiple_of(brick * BLOCK + t * TILE, HALF)
        pos = position_ref[:, pl.ds(node, TILE)] - 4.0
        norm = jnp.sum(pos * pos, axis=0, keepdims=True) + SOFTENING
        feat = jnp.where(sub == 3, norm, jnp.where(sub == 4, 1.0, 0.0))
        for i in range(3):
            feat = jnp.where(sub == i, pos[i : i + 1], feat)
        rows = jnp.concatenate([stack_six(feat, LEFT), jnp.zeros((HALF - 48, TILE), F32)], axis=0)
        left_ref[t * TILE : (t + 1) * TILE, :] = rows.T[:, :48].astype(BF16)


def prepare(place, position, moment):
    return pl.pallas_call(
        prepare_kernel,
        out_shape=(
            shaped(BLOCK, 48, dtype=BF16),
            shaped(48, SRC, dtype=BF16),
            shaped(8, SRC),
            shaped(8, HALF),
        ),
        in_specs=[SMEM, VMEM, VMEM],
        out_specs=(VMEM,) * 4,
        compiler_params=PARAMS,
        name="prepare",
    )(place, position, moment)


def layer_kernel(place_ref, left_ref, right_ref, moment_ref, trace_ref, fraction_ref, out_ref, acc):
    brick, row = place_ref[0], place_ref[1]
    acc[...] = jnp.zeros_like(acc)

    def chunk(c, carry):
        at = pl.multiple_of(c * CHUNK, CHUNK)
        trace = jnp.concatenate(
            [trace_ref[pl.ds(2 * c, 1), :], trace_ref[pl.ds(2 * c + 1, 1), :]], axis=1
        )
        face = moment_ref[:, pl.ds(at, CHUNK)] * trace
        face = stack_six(face, RIGHT).astype(BF16)
        dist = right_ref[:, pl.ds(at, CHUNK)]
        for t in range(1536 // TILE):
            rows = slice(t * TILE, (t + 1) * TILE)
            left = left_ref[rows, :]
            total = acc[rows, :]
            for n in range(CHUNK // 256):
                lanes = slice(n * 256, (n + 1) * 256)
                d = jnp.dot(left, dist[:, lanes], preferred_element_type=F32)
                f = jnp.dot(left, face[:, lanes], preferred_element_type=F32)
                r = lax.rsqrt(d)
                term = (f * r) * (r * r)
                total = total + term[:, :HALF] + term[:, HALF:]
            acc[rows, :] = total
        return carry

    lax.fori_loop(0, SRC // CHUNK, chunk, 0)
    for t in range(1536 // TILE):
        turned = acc[t * TILE : (t + 1) * TILE, :].T
        total = jnp.sum(turned, axis=0, keepdims=True)
        out_ref[:, t * TILE : (t + 1) * TILE] = total * (1.0 / (4.0 * math.pi))
    at = pl.multiple_of(row * 384, 128)
    own = (fraction_ref[...] - 1.0) * trace_ref[pl.ds(brick, 1), :]
    out_ref[:, pl.ds(at, 384)] = out_ref[:, pl.ds(at, 384)] + own


def layer(place, left, right, moment, traces, fraction):
    return pl.pallas_call(
        layer_kernel,
        out_shape=shaped(1, 1536),
        in_specs=[SMEM] + [VMEM] * 5,
        out_specs=VMEM,
        scratch_shapes=[pltpu.VMEM((1536, HALF), F32)],
        compiler_params=PARAMS,
        name="layer",
    )(place, left, right, moment, traces, fraction)


def answer_kernel(place_ref, part_ref, got_ref, out_ref, wide, table):
    row = place_ref[1]
    total = jnp.sum(part_ref[...], axis=0, keepdims=True)
    wide[...] = jnp.zeros_like(wide)
    lane = lax.broadcasted_iota(jnp.int32, (256, HALF), 1)
    wide[:, 0 : 3 * CAP] = got_ref[...]
    got = wide[...]
    slot = got.astype(jnp.int32)
    upper, lower = slot >> 7, slot & 127
    value = jnp.zeros((256, HALF), F32)
    for h in range(1536 // HALF):
        entry = jnp.broadcast_to(total[:, h * HALF : (h + 1) * HALF], (256, HALF))
        found = jnp.take_along_axis(entry, lower, axis=1)
        value = jnp.where(upper == h, found, value)
    cell = pltpu.roll(got, HALF - CAP, 1)
    pair = jnp.where(lane < CAP, value, jnp.where(lane < 2 * CAP, cell, 0.0))
    lane80 = lax.broadcasted_iota(jnp.int32, (80, HALF), 1)
    dead = jnp.where((lane80 >= CAP) & (lane80 < 2 * CAP), -1.0, 0.0)
    for q in range(6):
        table[q] = dead
    for q in range(4):
        table[q + 1, 8:72, :] = pair[q * 64 : (q + 1) * 64]
    for t in range(3):
        acc = jnp.zeros((64, HALF), F32)
        for s in range(5):
            piece = table[row + t, 6 + s : 70 + s, :]
            if s > 0:
                piece = pltpu.roll(piece, 2 * CAP * s, 1)
            acc = acc + piece
        out_ref[:, t * HALF : (t + 1) * HALF] = acc


def answer(place, partial, got):
    return pl.pallas_call(
        answer_kernel,
        out_shape=shaped(64, 384),
        in_specs=[SMEM, VMEM, VMEM],
        out_specs=VMEM,
        scratch_shapes=[pltpu.VMEM((256, HALF), F32), pltpu.VMEM((6, 80, HALF), F32)],
        compiler_params=PARAMS,
        name="answer",
    )(place, partial, got)


def second_kernel(place_ref, got_ref, first_ref, out_ref, mask, buf):
    brick, row = place_ref[0], place_ref[1]
    cells_x, cells_y = place_ref[2], place_ref[3]
    buf[0] = jnp.zeros((XD, YE, CZ), F32)
    z_at = lax.broadcasted_iota(jnp.int32, (CZ, HALF), 0)
    for t in range(3):
        block = got_ref[:, t * HALF : (t + 1) * HALF]
        turned = jnp.concatenate([block, pltpu.roll(block, HALF - 6, 1)], axis=0).T
        rows, begin = ((16, 0), (40, 8), (16, 40))[t]
        for s in range(5):
            planes, first_plane = ((4, 0), (8, 4), (8, 12), (8, 20), (4, 28))[s]
            x_off = 4 if s == 0 else 0
            hots, highs, lows = [], [], []
            row_at = lax.broadcasted_iota(jnp.int32, (planes * rows, HALF), 0)
            for k in range(6):
                value = turned[24 * s + k : 24 * s + k + 1, :]
                cell = turned[24 * s + CAP + k : 24 * s + CAP + k + 1, :].astype(jnp.int32)
                x = (cell >> 13) - x_off
                y = (cell >> 8) & 31
                live = (cell >= 0) & (x >= 0) & (x < planes)
                if t == 0:
                    live = live & (y >= 20)
                    y = y - 20
                else:
                    y = y + 4
                    if t == 2:
                        live = live & (y < 16)
                at = jnp.where(live, x * rows + y, -1)
                value = jnp.where(jnp.abs(value) < TINY, TINY, value)
                high = value.astype(BF16).astype(F32)
                hit = z_at == (cell & 255)
                hots.append(jnp.where(row_at == at, 1.0, 0.0).astype(BF16))
                highs.append(jnp.where(hit, high, 0.0).astype(BF16))
                lows.append(jnp.where(hit, value - high, 0.0).astype(BF16))
            hot = jnp.concatenate(hots, axis=1)
            total = None
            for part in (highs, lows):
                term = lax.dot_general(
                    hot, jnp.concatenate(part, axis=1), (((1,), (1,)), ((), ())), preferred_element_type=F32
                )
                total = term if total is None else total + term
            target = buf.at[0, first_plane : first_plane + planes, begin : begin + rows, :]
            target[...] = target[...] + total.reshape(planes, rows, CZ)
    y_at = lax.broadcasted_iota(jnp.int32, (YE, CZ), 0) + (row * CY - YO)
    in_y = (y_at >= 0) & (y_at < cells_y)

    def begin_plane(x, carry):
        v = buf[0, x]
        at = brick * CX + x - YO
        in_x = jnp.where((at >= 0) & (at < cells_x), 1.0, 0.0).astype(F32)
        mask[x] = jnp.where(in_y & (v == 0.0), in_x, 0.0)
        buf[0, x] = jnp.where(jnp.abs(v) < 2.0 * TINY, 0.0, v)
        return carry

    lax.fori_loop(0, XD, begin_plane, 0)
    for k in range(1, SWEEPS + 1):
        weight = WEIGHTS[k - 1]
        src, dst = buf.at[(k - 1) % 2], buf.at[k % 2]

        for x in range(k, XD - k):
            rows = plane_rows(SWEEPS - k - beside(x, YO, CX))
            begin, end = rows
            free = mask[x, begin:end, :]
            for h, (v, around) in enumerate(neighbours(src, x, rows)):
                lanes = slice(h * HALF, (h + 1) * HALF)
                dst[x, begin:end, lanes] = v + free[:, lanes] * ((weight / 6.0) * around - weight * v)
    for x in range(CX):
        out_ref[x] = first_ref[x] + buf[SWEEPS % 2, x + YO, YO : YO + CY, :]


def second_solve(place, got, first):
    return pl.pallas_call(
        second_kernel,
        out_shape=shaped(CX, CY, CZ),
        in_specs=[SMEM, VMEM, VMEM],
        out_specs=VMEM,
        scratch_shapes=[pltpu.VMEM((XD, YE, CZ), F32), pltpu.VMEM((2, XD, YE, CZ), F32)],
        compiler_params=PARAMS,
        name="second_solve",
    )(place, got, first)


def shifted(x, axis, step):
    count = lax.axis_size(axis)
    pairs = [(i, i + step) for i in range(count) if 0 <= i + step < count]
    return lax.ppermute(x, axis, pairs)


def local(
    magnet, node_position, node_moment, solid_fraction, request_cell, request_slot, request_count
):
    bricks, rows = lax.axis_size("brick"), lax.axis_size("row")
    brick, row = lax.axis_index("brick"), lax.axis_index("row")
    place = jnp.stack([brick, row, jnp.int32(bricks * CX), jnp.int32(rows * CY)]).astype(jnp.int32)
    cell, slot = request_cell[0, 0], request_slot[0, 0]
    live = jnp.arange(CAP)[None, :] < request_count[0, 0][:, None]
    zeros = jnp.zeros((bricks, CAP), F32)
    slot_f = jnp.where(live, slot, DEAD_SLOT).astype(F32)
    cell_f = jnp.where(live, cell, -1).astype(F32)
    base = jnp.concatenate([slot_f, zeros, cell_f], axis=1)
    cells = cell.T.reshape(2, 6, bricks).transpose(1, 0, 2).reshape(6, 2 * bricks)
    fraction = lax.dynamic_slice_in_dim(solid_fraction, brick * 1536 + row * 384, 384, 0)[None]
    left, right, moment, order = prepare(place, node_position, node_moment)

    own, flat, low, high = own_source(magnet)
    l1, r1 = shifted(flat, "brick", 1), shifted(flat, "brick", -1)
    l2, r2 = shifted(high, "brick", 2), shifted(low, "brick", -2)
    sx, upper, lower = join_x(own, l1, r1, l2, r2, order)
    below, above = shifted(upper, "row", 1), shifted(lower, "row", -1)
    first, message = first_solve(place, sx, below, above, cells, base)
    message = message.reshape(rows * bricks, 3 * CAP)
    got = lax.all_to_all(message, ("row", "brick"), split_axis=0, concat_axis=0, tiled=True)
    quarter = place_quarter(place, got)
    traces = lax.all_to_all(quarter, "brick", split_axis=0, concat_axis=0, tiled=True)
    partial = layer(place, left, right, moment, traces, fraction)
    partials = lax.all_gather(partial, "row", axis=0, tiled=True)
    reply = answer(place, partials, got)
    returned = lax.all_to_all(reply, "brick", split_axis=0, concat_axis=0, tiled=True)
    potential = second_solve(place, returned, first)
    begin = HALF + 2 * 2 * CAP
    boundary = jnp.where(live, returned[:, begin : begin + CAP], 0.0)
    return potential, boundary[None, None]


def solution(mesh):
    placed = (
        P(None, "brick", "row", None),
        P(),
        P(),
        P(),
        P("brick", "row", None, None),
        P("brick", "row", None, None),
        P("brick", "row", None),
    )
    return jax.shard_map(
        local,
        mesh=mesh,
        in_specs=placed,
        out_specs=(P("brick", "row", None), P("brick", "row", None, None)),
        check_vma=False,
    )
```

```python
import functools
import math

import jax
import jax.numpy as jnp
from jax import lax
from jax.experimental import pallas as pl
from jax.experimental.pallas import tpu as pltpu
from jax.sharding import PartitionSpec as P

CX = 8
CY = 32
CZ = 256
SWEEPS = 12
CAP = 12
RELAX_LOW = 0.5
RELAX_HIGH = 2.0
SOFTENING = 0.5

YO = 12
YE = CY + 24
XS = CX + 22
XD = CX + 24
HALF = 128
RIM = CY + 2
PARAMS = pltpu.CompilerParams(vmem_limit_bytes=50 * 1024 * 1024)
DEAD_SLOT = 4096
TINY = 1e-30
F32 = jnp.float32
BF16 = jnp.bfloat16
VMEM = pl.BlockSpec(memory_space=pltpu.VMEM)
SMEM = pl.BlockSpec(memory_space=pltpu.SMEM)


def sweep_weights(total_steps):
    centre = 0.5 * (RELAX_HIGH + RELAX_LOW)
    radius = 0.5 * (RELAX_HIGH - RELAX_LOW)
    root_list = [
        1.0 / (centre + radius * math.cos(math.pi * (2 * order_index + 1) / (2 * total_steps)))
        for order_index in range(total_steps)
    ]
    ordered = []
    for order_index in range(total_steps // 2):
        ordered.append(root_list[order_index])
        ordered.append(root_list[total_steps - 1 - order_index])
    return ordered


WEIGHTS = sweep_weights(SWEEPS)


def shaped(*dims, dtype=F32):
    return jax.ShapeDtypeStruct(dims, dtype)


def split3(v):
    hi = v.astype(BF16).astype(F32)
    rest = v - hi
    mid = rest.astype(BF16).astype(F32)
    return hi, mid, rest - mid


def z_pair(left, right):
    lane = lax.broadcasted_iota(jnp.int32, left.shape, 1)
    left_dn = pltpu.roll(left, 1, 1)
    right_dn = pltpu.roll(right, 1, 1)
    left_up = pltpu.roll(left, HALF - 1, 1)
    right_up = pltpu.roll(right, HALF - 1, 1)
    first, last = lane == 0, lane == HALF - 1
    dn = (jnp.where(first, 0.0, left_dn), jnp.where(first, left_dn, right_dn))
    up = (jnp.where(last, right_up, left_up), jnp.where(last, 0.0, right_up))
    return dn, up


def source_kernel(m_ref, e_ref, flat_ref, low_ref, high_ref, pad):
    pad[...] = jnp.zeros_like(pad)
    for x in range(CX):
        pad[0, x + 1, 12:44, :] = m_ref[0, x]
        pad[1, x + 1, 12:44, :] = m_ref[1, x]
        pad[2, x + 1, 12:44, :] = m_ref[2, x]
    zeros = jnp.zeros((40, CZ), F32)
    for i in range(CX + 2):
        ahead = pad[0, i + 1, 8:48, :] if i + 1 <= CX else zeros
        behind = pad[0, i - 1, 8:48, :] if i >= 2 else zeros
        total = ahead - behind
        if 1 <= i <= CX:
            total = total + (pad[1, i, 9:49, :] - pad[1, i, 7:47, :])
            c = pad[2, i, 8:48, :]
            dn, up = z_pair(c[:, :HALF], c[:, HALF:])
            total = total + jnp.concatenate([up[0] - dn[0], up[1] - dn[1]], axis=1)
        total = -0.5 * total
        e_ref[i] = total
        rim = e_ref[i, 3:37, :]
        flat_ref[i * RIM : (i + 1) * RIM, :] = rim
        if i < 4:
            low_ref[i * RIM : (i + 1) * RIM, :] = rim
        j = i - (CX - 2)
        if j >= 0:
            high_ref[j * RIM : (j + 1) * RIM, :] = rim


def own_source(magnet):
    return pl.pallas_call(
        source_kernel,
        out_shape=(
            shaped(10, 40, CZ),
            shaped(10 * RIM, CZ),
            shaped(4 * RIM, CZ),
            shaped(4 * RIM, CZ),
        ),
        in_specs=[VMEM],
        out_specs=(VMEM,) * 4,
        scratch_shapes=[pltpu.VMEM((3, CX + 2, 56, CZ), F32)],
        compiler_params=PARAMS,
        name="own_source",
    )(magnet)


def beside(plane, before, own):
    return max(before - plane, plane - (before + own - 1), 0)


def y_rows():
    counts = [CX + 4 - beside(plane, 11, CX) for plane in range(XS)]
    begins = [sum(counts[:plane]) for plane in range(XS)]
    return counts, begins, -(-sum(counts) // 8) * 8


Y_COUNTS, Y_BEGINS, Y_TOTAL = y_rows()


def join_kernel(e_ref, l1_ref, r1_ref, l2_ref, r2_ref, order_ref, sx_ref, upper_ref, lower_ref):
    del order_ref
    parts = ((l1_ref, 2, 10), (r1_ref, 18, 10), (l2_ref, 0, 4), (r2_ref, 26, 4))
    upper_ref[Y_TOTAL - 8 :, :] = jnp.zeros((8, CZ), F32)
    lower_ref[Y_TOTAL - 8 :, :] = jnp.zeros((8, CZ), F32)
    for plane in range(XS):
        own = 10 <= plane < 20
        sx_ref[plane] = e_ref[plane - 10] if own else jnp.zeros((40, CZ), F32)
        total = sx_ref[plane, 3:37, :] if own else None
        for ref, begin, count in parts:
            if begin <= plane < begin + count:
                at = (plane - begin) * RIM
                term = ref[at : at + RIM, :]
                total = term if total is None else total + term
        sx_ref[plane, 3:37, :] = total
        rows, at = Y_COUNTS[plane], Y_BEGINS[plane]
        upper_ref[at : at + rows, :] = sx_ref[plane, 37 - rows : 37, :]
        lower_ref[at : at + rows, :] = sx_ref[plane, 3 : 3 + rows, :]


def join_x(own, l1, r1, l2, r2, order):
    return pl.pallas_call(
        join_kernel,
        out_shape=(shaped(XS, 40, CZ), shaped(Y_TOTAL, CZ), shaped(Y_TOTAL, CZ)),
        in_specs=[VMEM] * 6,
        out_specs=(VMEM,) * 3,
        compiler_params=PARAMS,
        name="join_x",
    )(own, l1, r1, l2, r2, order)


def plane_rows(reach):
    return (0, YE) if reach > 3 else (8, YE - 8)


def neighbours(src, x, rows):
    begin, end = rows
    c = src[x, begin:end, :]
    around_x = src[x - 1, begin:end, :] + src[x + 1, begin:end, :]
    halves = (c[:, :HALF], c[:, HALF:])
    dn, up = z_pair(*halves)
    out = []
    for h in range(2):
        v = halves[h]
        around_y = pltpu.roll(v, 1, 0) + pltpu.roll(v, end - begin - 1, 0)
        around = around_x[:, h * HALF : (h + 1) * HALF] + around_y + (dn[h] + up[h])
        out.append((v, around))
    return out


def first_kernel(place_ref, sx_ref, below_ref, above_ref, cell_ref, base_ref, field_ref, msg_ref, s, buf):
    brick, row = place_ref[0], place_ref[1]
    cells_x, cells_y = place_ref[2], place_ref[3]
    y_at = lax.broadcasted_iota(jnp.int32, (YE, HALF), 0) + (row * CY - YO)
    in_y = jnp.where((y_at >= 0) & (y_at < cells_y), 1.0, 0.0).astype(F32)

    def x_scale(x, scale):
        at = brick * CX + x - 11
        return jnp.where((at >= 0) & (at < cells_x), scale, 0.0).astype(F32)

    edge = jnp.zeros((8, CZ), F32)
    for x in range(XS):
        s[x, 0:8, :] = edge
        s[x, 48:56, :] = edge
        s[x, 8:48, :] = sx_ref[x]
        rows, at = Y_COUNTS[x], Y_BEGINS[x]
        s[x, 13 - rows : 13, :] += below_ref[at : at + rows, :]
        s[x, 43 : 43 + rows, :] += above_ref[at : at + rows, :]
        coef = in_y * x_scale(x, WEIGHTS[0] / 6.0)
        full = s[x]
        buf[0, x, :, :HALF] = coef * full[:, :HALF]
        buf[0, x, :, HALF:] = coef * full[:, HALF:]
    for k in range(1, SWEEPS):
        weight = WEIGHTS[k]
        src, dst = buf.at[(k - 1) % 2], buf.at[k % 2]

        for x in range(k, XS - k):
            rows = plane_rows(SWEEPS - 1 - k - beside(x, 11, CX))
            begin, end = rows
            coef = in_y[begin:end] * x_scale(x, weight / 6.0)
            source = s[x, begin:end, :]
            for h, (v, around) in enumerate(neighbours(src, x, rows)):
                lanes = slice(h * HALF, (h + 1) * HALF)
                dst[x, begin:end, lanes] = (1.0 - weight) * v + coef * (source[:, lanes] + around)
    last = (SWEEPS - 1) % 2
    for x in range(CX):
        field_ref[x] = buf[last, x + 11, YO : YO + CY, :]
    flat = field_ref[...].reshape(CX * CY, CZ)
    turned = flat.T
    parts = [p.astype(BF16) for p in split3(turned)]
    row_at = lax.broadcasted_iota(jnp.int32, (CX * CY, HALF), 0)
    picked = []
    for k in range(6):
        cell = cell_ref[k : k + 1, :]
        hot = jnp.where(row_at == (cell >> 8), 1.0, 0.0).astype(BF16)
        at_rows = sum(jnp.dot(p, hot, preferred_element_type=F32) for p in parts)
        kept = jnp.where(row_at == (cell & 255), at_rows, 0.0)
        picked.append(jnp.sum(kept, axis=0, keepdims=True))
    sub = lax.broadcasted_iota(jnp.int32, (HALF, HALF), 0)
    tile = jnp.zeros((HALF, HALF), F32)
    for k in range(6):
        tile = jnp.where(sub == k, picked[k], tile)
    turned_tile = tile.T
    both = turned_tile[0:64] + pltpu.roll(turned_tile[64:128], 6, 1)
    traces = pltpu.roll(both, CAP, 1)
    lanes = 3 * CAP
    full = base_ref[...] + traces[:, :lanes]
    for q in range(4):
        msg_ref[q] = full


def first_solve(place, sx, below, above, cells, base):
    return pl.pallas_call(
        first_kernel,
        out_shape=(shaped(CX, CY, CZ), shaped(4, 64, 3 * CAP)),
        in_specs=[SMEM] + [VMEM] * 5,
        out_specs=(VMEM, VMEM),
        scratch_shapes=[pltpu.VMEM((XS, YE, CZ), F32), pltpu.VMEM((2, XS, YE, CZ), F32)],
        compiler_params=PARAMS,
        name="first_solve",
    )(place, sx, below, above, cells, base)


def place_kernel(place_ref, got_ref, out_ref):
    row = place_ref[1]
    got = got_ref[...]
    at = (lax.broadcasted_iota(jnp.int32, (256, 384), 1) + row * 384).astype(F32)
    acc = jnp.zeros((256, 384), F32)
    for i in range(CAP):
        slot = got[:, i : i + 1]
        trace = got[:, CAP + i : CAP + i + 1]
        acc = acc + jnp.where(at == slot, trace, 0.0)
    total = jnp.sum(acc, axis=0, keepdims=True)
    out_ref[...] = jnp.broadcast_to(total, (64, 384))


def place_quarter(place, got):
    return pl.pallas_call(
        place_kernel,
        out_shape=shaped(64, 384),
        in_specs=[SMEM, VMEM],
        out_specs=VMEM,
        compiler_params=PARAMS,
        name="place_quarter",
    )(place, got)


SRC = 24576
BLOCK = 1536
QUARTER = 384
CHUNK = 768
TILE = 128


def stack_six(v, order):
    parts = split3(v)
    return jnp.concatenate([parts[i] for i in order], axis=0)


RIGHT = (0, 1, 2, 0, 1, 0)
LEFT = (0, 0, 0, 1, 1, 2)


def prepare_kernel(place_ref, position_ref, moment_ref, right_ref, face_ref, order_ref):
    row = place_ref[1]
    sub = lax.broadcasted_iota(jnp.int32, (8, QUARTER), 0)
    order_ref[...] = jnp.zeros((8, HALF), F32)

    def sources(b, carry):
        node = pl.multiple_of(b * BLOCK + row * QUARTER, HALF)
        at = pl.multiple_of(b * QUARTER, HALF)
        pos = position_ref[:, pl.ds(node, QUARTER)] - 4.0
        mom = moment_ref[:, pl.ds(node, QUARTER)]
        norm = jnp.sum(pos * pos, axis=0, keepdims=True)
        across = jnp.sum(pos * mom, axis=0, keepdims=True)
        dist = jnp.where(sub == 3, 1.0, jnp.where(sub == 4, norm, 0.0))
        face = jnp.where(sub == 4, -across, 0.0)
        for i in range(3):
            dist = jnp.where(sub == i, -2.0 * pos[i : i + 1], dist)
            face = jnp.where(sub == i, mom[i : i + 1], face)
        right_ref[:, pl.ds(at, QUARTER)] = stack_six(dist, RIGHT).astype(BF16)
        face_ref[:, pl.ds(at, QUARTER)] = face
        return carry

    lax.fori_loop(0, SRC // QUARTER, sources, 0, unroll=2)


def prepare(place, position, moment):
    return pl.pallas_call(
        prepare_kernel,
        out_shape=(
            shaped(48, SRC, dtype=BF16),
            shaped(8, SRC),
            shaped(8, HALF),
        ),
        in_specs=[SMEM, VMEM, VMEM],
        out_specs=(VMEM,) * 3,
        compiler_params=PARAMS,
        name="prepare",
    )(place, position, moment)


def targets_kernel(target_ref, left_ref):
    sub = lax.broadcasted_iota(jnp.int32, (8, TILE), 0)
    for t in range(BLOCK // TILE):
        pos = target_ref[:, t * TILE : (t + 1) * TILE] - 4.0
        norm = jnp.sum(pos * pos, axis=0, keepdims=True) + SOFTENING
        feat = jnp.where(sub == 3, norm, jnp.where(sub == 4, 1.0, 0.0))
        for i in range(3):
            feat = jnp.where(sub == i, pos[i : i + 1], feat)
        rows = jnp.concatenate([stack_six(feat, LEFT), jnp.zeros((HALF - 48, TILE), F32)], axis=0)
        left_ref[t * TILE : (t + 1) * TILE, :] = rows.T[:, :48].astype(BF16)


def prepare_targets(targets):
    return pl.pallas_call(
        targets_kernel,
        out_shape=shaped(BLOCK, 48, dtype=BF16),
        in_specs=[VMEM],
        out_specs=VMEM,
        compiler_params=PARAMS,
        name="prepare_targets",
    )(targets)


def layer_kernel(place_ref, left_ref, right_ref, moment_ref, trace_ref, fraction_ref, out_ref, acc):
    brick, row = place_ref[0], place_ref[1]
    acc[...] = jnp.zeros_like(acc)

    def chunk(c, carry):
        at = pl.multiple_of(c * CHUNK, CHUNK)
        trace = jnp.concatenate(
            [trace_ref[pl.ds(2 * c, 1), :], trace_ref[pl.ds(2 * c + 1, 1), :]], axis=1
        )
        face = moment_ref[:, pl.ds(at, CHUNK)] * trace
        face = stack_six(face, RIGHT).astype(BF16)
        dist = right_ref[:, pl.ds(at, CHUNK)]
        for t in range(1536 // TILE):
            rows = slice(t * TILE, (t + 1) * TILE)
            left = left_ref[rows, :]
            total = acc[rows, :]
            for n in range(CHUNK // 256):
                lanes = slice(n * 256, (n + 1) * 256)
                d = jnp.dot(left, dist[:, lanes], preferred_element_type=F32)
                f = jnp.dot(left, face[:, lanes], preferred_element_type=F32)
                r = lax.rsqrt(d)
                term = (f * r) * (r * r)
                total = total + term[:, :HALF] + term[:, HALF:]
            acc[rows, :] = total
        return carry

    lax.fori_loop(0, SRC // CHUNK, chunk, 0)
    for t in range(1536 // TILE):
        turned = acc[t * TILE : (t + 1) * TILE, :].T
        total = jnp.sum(turned, axis=0, keepdims=True)
        out_ref[:, t * TILE : (t + 1) * TILE] = total * (1.0 / (4.0 * math.pi))
    at = pl.multiple_of(row * 384, 128)
    own = (fraction_ref[...] - 1.0) * trace_ref[pl.ds(brick, 1), :]
    out_ref[:, pl.ds(at, 384)] = out_ref[:, pl.ds(at, 384)] + own


def layer(place, left, right, moment, traces, fraction):
    return pl.pallas_call(
        layer_kernel,
        out_shape=shaped(1, 1536),
        in_specs=[SMEM] + [VMEM] * 5,
        out_specs=VMEM,
        scratch_shapes=[pltpu.VMEM((1536, HALF), F32)],
        compiler_params=PARAMS,
        name="layer",
    )(place, left, right, moment, traces, fraction)


def answer_kernel(place_ref, part_ref, got_ref, out_ref, wide, table):
    row = place_ref[1]
    total = jnp.sum(part_ref[...], axis=0, keepdims=True)
    wide[...] = jnp.zeros_like(wide)
    lane = lax.broadcasted_iota(jnp.int32, (256, HALF), 1)
    wide[:, 0 : 3 * CAP] = got_ref[...]
    got = wide[...]
    slot = got.astype(jnp.int32)
    upper, lower = slot >> 7, slot & 127
    value = jnp.zeros((256, HALF), F32)
    for h in range(1536 // HALF):
        entry = jnp.broadcast_to(total[:, h * HALF : (h + 1) * HALF], (256, HALF))
        found = jnp.take_along_axis(entry, lower, axis=1)
        value = jnp.where(upper == h, found, value)
    cell = pltpu.roll(got, HALF - CAP, 1)
    pair = jnp.where(lane < CAP, value, jnp.where(lane < 2 * CAP, cell, 0.0))
    lane80 = lax.broadcasted_iota(jnp.int32, (80, HALF), 1)
    dead = jnp.where((lane80 >= CAP) & (lane80 < 2 * CAP), -1.0, 0.0)
    for q in range(6):
        table[q] = dead
    for q in range(4):
        table[q + 1, 8:72, :] = pair[q * 64 : (q + 1) * 64]
    for t in range(3):
        acc = jnp.zeros((64, HALF), F32)
        for s in range(5):
            piece = table[row + t, 6 + s : 70 + s, :]
            if s > 0:
                piece = pltpu.roll(piece, 2 * CAP * s, 1)
            acc = acc + piece
        out_ref[:, t * HALF : (t + 1) * HALF] = acc


def answer(place, partial, got):
    return pl.pallas_call(
        answer_kernel,
        out_shape=shaped(64, 384),
        in_specs=[SMEM, VMEM, VMEM],
        out_specs=VMEM,
        scratch_shapes=[pltpu.VMEM((256, HALF), F32), pltpu.VMEM((6, 80, HALF), F32)],
        compiler_params=PARAMS,
        name="answer",
    )(place, partial, got)


def second_kernel(place_ref, got_ref, first_ref, out_ref, mask, buf):
    brick, row = place_ref[0], place_ref[1]
    cells_x, cells_y = place_ref[2], place_ref[3]
    buf[0] = jnp.zeros((XD, YE, CZ), F32)
    z_at = lax.broadcasted_iota(jnp.int32, (CZ, HALF), 0)
    for t in range(3):
        block = got_ref[:, t * HALF : (t + 1) * HALF]
        turned = jnp.concatenate([block, pltpu.roll(block, HALF - 6, 1)], axis=0).T
        rows, begin = ((16, 0), (40, 8), (16, 40))[t]
        for s in range(5):
            planes, first_plane = ((4, 0), (8, 4), (8, 12), (8, 20), (4, 28))[s]
            x_off = 4 if s == 0 else 0
            hots, highs, lows = [], [], []
            row_at = lax.broadcasted_iota(jnp.int32, (planes * rows, HALF), 0)
            for k in range(6):
                value = turned[24 * s + k : 24 * s + k + 1, :]
                cell = turned[24 * s + CAP + k : 24 * s + CAP + k + 1, :].astype(jnp.int32)
                x = (cell >> 13) - x_off
                y = (cell >> 8) & 31
                live = (cell >= 0) & (x >= 0) & (x < planes)
                if t == 0:
                    live = live & (y >= 20)
                    y = y - 20
                else:
                    y = y + 4
                    if t == 2:
                        live = live & (y < 16)
                at = jnp.where(live, x * rows + y, -1)
                value = jnp.where(jnp.abs(value) < TINY, TINY, value)
                high = value.astype(BF16).astype(F32)
                hit = z_at == (cell & 255)
                hots.append(jnp.where(row_at == at, 1.0, 0.0).astype(BF16))
                highs.append(jnp.where(hit, high, 0.0).astype(BF16))
                lows.append(jnp.where(hit, value - high, 0.0).astype(BF16))
            hot = jnp.concatenate(hots, axis=1)
            total = None
            for part in (highs, lows):
                term = lax.dot_general(
                    hot, jnp.concatenate(part, axis=1), (((1,), (1,)), ((), ())), preferred_element_type=F32
                )
                total = term if total is None else total + term
            target = buf.at[0, first_plane : first_plane + planes, begin : begin + rows, :]
            target[...] = target[...] + total.reshape(planes, rows, CZ)
    y_at = lax.broadcasted_iota(jnp.int32, (YE, CZ), 0) + (row * CY - YO)
    in_y = (y_at >= 0) & (y_at < cells_y)

    def begin_plane(x, carry):
        v = buf[0, x]
        at = brick * CX + x - YO
        in_x = jnp.where((at >= 0) & (at < cells_x), 1.0, 0.0).astype(F32)
        mask[x] = jnp.where(in_y & (v == 0.0), in_x, 0.0)
        buf[0, x] = jnp.where(jnp.abs(v) < 2.0 * TINY, 0.0, v)
        return carry

    lax.fori_loop(0, XD, begin_plane, 0)
    for k in range(1, SWEEPS + 1):
        weight = WEIGHTS[k - 1]
        src, dst = buf.at[(k - 1) % 2], buf.at[k % 2]

        for x in range(k, XD - k):
            rows = plane_rows(SWEEPS - k - beside(x, YO, CX))
            begin, end = rows
            free = mask[x, begin:end, :]
            for h, (v, around) in enumerate(neighbours(src, x, rows)):
                lanes = slice(h * HALF, (h + 1) * HALF)
                dst[x, begin:end, lanes] = v + free[:, lanes] * ((weight / 6.0) * around - weight * v)
    for x in range(CX):
        out_ref[x] = first_ref[x] + buf[SWEEPS % 2, x + YO, YO : YO + CY, :]


def second_solve(place, got, first):
    return pl.pallas_call(
        second_kernel,
        out_shape=shaped(CX, CY, CZ),
        in_specs=[SMEM, VMEM, VMEM],
        out_specs=VMEM,
        scratch_shapes=[pltpu.VMEM((XD, YE, CZ), F32), pltpu.VMEM((2, XD, YE, CZ), F32)],
        compiler_params=PARAMS,
        name="second_solve",
    )(place, got, first)


def shifted(x, axis, step):
    count = lax.axis_size(axis)
    pairs = [(i, i + step) for i in range(count) if 0 <= i + step < count]
    return lax.ppermute(x, axis, pairs)


def local(
    magnet, node_position, node_moment, solid_fraction, request_cell, request_slot, request_count
):
    bricks, rows = lax.axis_size("brick"), lax.axis_size("row")
    brick, row = lax.axis_index("brick"), lax.axis_index("row")
    place = jnp.stack([brick, row, jnp.int32(bricks * CX), jnp.int32(rows * CY)]).astype(jnp.int32)
    cell, slot = request_cell[0, 0], request_slot[0, 0]
    live = jnp.arange(CAP)[None, :] < request_count[0, 0][:, None]
    zeros = jnp.zeros((bricks, CAP), F32)
    slot_f = jnp.where(live, slot, DEAD_SLOT).astype(F32)
    cell_f = jnp.where(live, cell, -1).astype(F32)
    base = jnp.concatenate([slot_f, zeros, cell_f], axis=1)
    cells = cell.T.reshape(2, 6, bricks).transpose(1, 0, 2).reshape(6, 2 * bricks)
    fraction = lax.dynamic_slice_in_dim(solid_fraction, brick * 1536 + row * 384, 384, 0)[None]
    right, moment, order = prepare(place, node_position, node_moment)
    targets = lax.dynamic_slice_in_dim(node_position, brick * BLOCK, BLOCK, 1)
    left = prepare_targets(targets)

    own, flat, low, high = own_source(magnet)
    l1, r1 = shifted(flat, "brick", 1), shifted(flat, "brick", -1)
    l2, r2 = shifted(high, "brick", 2), shifted(low, "brick", -2)
    sx, upper, lower = join_x(own, l1, r1, l2, r2, order)
    below, above = shifted(upper, "row", 1), shifted(lower, "row", -1)
    first, message = first_solve(place, sx, below, above, cells, base)
    message = message.reshape(rows * bricks, 3 * CAP)
    got = lax.all_to_all(message, ("row", "brick"), split_axis=0, concat_axis=0, tiled=True)
    quarter = place_quarter(place, got)
    traces = lax.all_to_all(quarter, "brick", split_axis=0, concat_axis=0, tiled=True)
    partial = layer(place, left, right, moment, traces, fraction)
    partials = lax.all_gather(partial, "row", axis=0, tiled=True)
    reply = answer(place, partials, got)
    returned = lax.all_to_all(reply, "brick", split_axis=0, concat_axis=0, tiled=True)
    potential = second_solve(place, returned, first)
    begin = HALF + 2 * 2 * CAP
    boundary = jnp.where(live, returned[:, begin : begin + CAP], 0.0)
    return potential, boundary[None, None]


def solution(mesh):
    placed = (
        P(None, "brick", "row", None),
        P(),
        P(),
        P(),
        P("brick", "row", None, None),
        P("brick", "row", None, None),
        P("brick", "row", None),
    )
    return jax.shard_map(
        local,
        mesh=mesh,
        in_specs=placed,
        out_specs=(P("brick", "row", None), P("brick", "row", None, None)),
        check_vma=False,
    )
```

```python
import functools
import math

import jax
import jax.numpy as jnp
from jax import lax
from jax.experimental import pallas as pl
from jax.experimental.pallas import tpu as pltpu
from jax.sharding import PartitionSpec as P

CX = 8
CY = 32
CZ = 256
SWEEPS = 12
CAP = 12
RELAX_LOW = 0.5
RELAX_HIGH = 2.0
SOFTENING = 0.5

YO = 12
YE = CY + 24
XS = CX + 22
XD = CX + 24
HALF = 128
RIM = CY + 2
PARAMS = pltpu.CompilerParams(vmem_limit_bytes=50 * 1024 * 1024)
DEAD_SLOT = 4096
TINY = 1e-30
F32 = jnp.float32
BF16 = jnp.bfloat16
VMEM = pl.BlockSpec(memory_space=pltpu.VMEM)
SMEM = pl.BlockSpec(memory_space=pltpu.SMEM)


def sweep_weights(total_steps):
    centre = 0.5 * (RELAX_HIGH + RELAX_LOW)
    radius = 0.5 * (RELAX_HIGH - RELAX_LOW)
    root_list = [
        1.0 / (centre + radius * math.cos(math.pi * (2 * order_index + 1) / (2 * total_steps)))
        for order_index in range(total_steps)
    ]
    ordered = []
    for order_index in range(total_steps // 2):
        ordered.append(root_list[order_index])
        ordered.append(root_list[total_steps - 1 - order_index])
    return ordered


WEIGHTS = sweep_weights(SWEEPS)


def shaped(*dims, dtype=F32):
    return jax.ShapeDtypeStruct(dims, dtype)


def split3(v):
    hi = v.astype(BF16).astype(F32)
    rest = v - hi
    mid = rest.astype(BF16).astype(F32)
    return hi, mid, rest - mid


def z_pair(left, right):
    lane = lax.broadcasted_iota(jnp.int32, left.shape, 1)
    left_dn = pltpu.roll(left, 1, 1)
    right_dn = pltpu.roll(right, 1, 1)
    left_up = pltpu.roll(left, HALF - 1, 1)
    right_up = pltpu.roll(right, HALF - 1, 1)
    first, last = lane == 0, lane == HALF - 1
    dn = (jnp.where(first, 0.0, left_dn), jnp.where(first, left_dn, right_dn))
    up = (jnp.where(last, right_up, left_up), jnp.where(last, 0.0, right_up))
    return dn, up


def source_kernel(m_ref, e_ref, flat_ref, low_ref, high_ref, pad):
    pad[...] = jnp.zeros_like(pad)
    for x in range(CX):
        pad[0, x + 1, 12:44, :] = m_ref[0, x]
        pad[1, x + 1, 12:44, :] = m_ref[1, x]
        pad[2, x + 1, 12:44, :] = m_ref[2, x]
    zeros = jnp.zeros((40, CZ), F32)
    for i in range(CX + 2):
        ahead = pad[0, i + 1, 8:48, :] if i + 1 <= CX else zeros
        behind = pad[0, i - 1, 8:48, :] if i >= 2 else zeros
        total = ahead - behind
        if 1 <= i <= CX:
            total = total + (pad[1, i, 9:49, :] - pad[1, i, 7:47, :])
            c = pad[2, i, 8:48, :]
            dn, up = z_pair(c[:, :HALF], c[:, HALF:])
            total = total + jnp.concatenate([up[0] - dn[0], up[1] - dn[1]], axis=1)
        total = -0.5 * total
        e_ref[i] = total
        rim = e_ref[i, 3:37, :]
        flat_ref[i * RIM : (i + 1) * RIM, :] = rim
        if i < 4:
            low_ref[i * RIM : (i + 1) * RIM, :] = rim
        j = i - (CX - 2)
        if j >= 0:
            high_ref[j * RIM : (j + 1) * RIM, :] = rim


def own_source(magnet):
    return pl.pallas_call(
        source_kernel,
        out_shape=(
            shaped(10, 40, CZ),
            shaped(10 * RIM, CZ),
            shaped(4 * RIM, CZ),
            shaped(4 * RIM, CZ),
        ),
        in_specs=[VMEM],
        out_specs=(VMEM,) * 4,
        scratch_shapes=[pltpu.VMEM((3, CX + 2, 56, CZ), F32)],
        compiler_params=PARAMS,
        name="own_source",
    )(magnet)


def beside(plane, before, own):
    return max(before - plane, plane - (before + own - 1), 0)


def y_rows():
    counts = [CX + 4 - beside(plane, 11, CX) for plane in range(XS)]
    begins = [sum(counts[:plane]) for plane in range(XS)]
    return counts, begins, -(-sum(counts) // 8) * 8


Y_COUNTS, Y_BEGINS, Y_TOTAL = y_rows()


def join_kernel(e_ref, l1_ref, r1_ref, l2_ref, r2_ref, order_ref, sx_ref, upper_ref, lower_ref):
    del order_ref
    parts = ((l1_ref, 2, 10), (r1_ref, 18, 10), (l2_ref, 0, 4), (r2_ref, 26, 4))
    upper_ref[Y_TOTAL - 8 :, :] = jnp.zeros((8, CZ), F32)
    lower_ref[Y_TOTAL - 8 :, :] = jnp.zeros((8, CZ), F32)
    for plane in range(XS):
        own = 10 <= plane < 20
        sx_ref[plane] = e_ref[plane - 10] if own else jnp.zeros((40, CZ), F32)
        total = sx_ref[plane, 3:37, :] if own else None
        for ref, begin, count in parts:
            if begin <= plane < begin + count:
                at = (plane - begin) * RIM
                term = ref[at : at + RIM, :]
                total = term if total is None else total + term
        sx_ref[plane, 3:37, :] = total
        rows, at = Y_COUNTS[plane], Y_BEGINS[plane]
        upper_ref[at : at + rows, :] = sx_ref[plane, 37 - rows : 37, :]
        lower_ref[at : at + rows, :] = sx_ref[plane, 3 : 3 + rows, :]


def join_x(own, l1, r1, l2, r2, order):
    return pl.pallas_call(
        join_kernel,
        out_shape=(shaped(XS, 40, CZ), shaped(Y_TOTAL, CZ), shaped(Y_TOTAL, CZ)),
        in_specs=[VMEM] * 6,
        out_specs=(VMEM,) * 3,
        compiler_params=PARAMS,
        name="join_x",
    )(own, l1, r1, l2, r2, order)


def plane_rows(reach):
    return (0, YE) if reach > 3 else (8, YE - 8)


def neighbours(src, x, rows):
    begin, end = rows
    c = src[x, begin:end, :]
    around_x = src[x - 1, begin:end, :] + src[x + 1, begin:end, :]
    halves = (c[:, :HALF], c[:, HALF:])
    dn, up = z_pair(*halves)
    out = []
    for h in range(2):
        v = halves[h]
        around_y = pltpu.roll(v, 1, 0) + pltpu.roll(v, end - begin - 1, 0)
        around = around_x[:, h * HALF : (h + 1) * HALF] + around_y + (dn[h] + up[h])
        out.append((v, around))
    return out


def first_kernel(place_ref, sx_ref, below_ref, above_ref, cell_ref, base_ref, field_ref, msg_ref, s, buf):
    brick, row = place_ref[0], place_ref[1]
    cells_x, cells_y = place_ref[2], place_ref[3]
    y_at = lax.broadcasted_iota(jnp.int32, (YE, HALF), 0) + (row * CY - YO)
    in_y = jnp.where((y_at >= 0) & (y_at < cells_y), 1.0, 0.0).astype(F32)

    def x_scale(x, scale):
        at = brick * CX + x - 11
        return jnp.where((at >= 0) & (at < cells_x), scale, 0.0).astype(F32)

    edge = jnp.zeros((8, CZ), F32)
    for x in range(XS):
        s[x, 0:8, :] = edge
        s[x, 48:56, :] = edge
        s[x, 8:48, :] = sx_ref[x]
        rows, at = Y_COUNTS[x], Y_BEGINS[x]
        s[x, 13 - rows : 13, :] += below_ref[at : at + rows, :]
        s[x, 43 : 43 + rows, :] += above_ref[at : at + rows, :]
        coef = in_y * x_scale(x, WEIGHTS[0] / 6.0)
        full = s[x]
        buf[0, x, :, :HALF] = coef * full[:, :HALF]
        buf[0, x, :, HALF:] = coef * full[:, HALF:]
    for k in range(1, SWEEPS):
        weight = WEIGHTS[k]
        src, dst = buf.at[(k - 1) % 2], buf.at[k % 2]

        for x in range(k, XS - k):
            rows = plane_rows(SWEEPS - 1 - k - beside(x, 11, CX))
            begin, end = rows
            coef = in_y[begin:end] * x_scale(x, weight / 6.0)
            source = s[x, begin:end, :]
            for h, (v, around) in enumerate(neighbours(src, x, rows)):
                lanes = slice(h * HALF, (h + 1) * HALF)
                dst[x, begin:end, lanes] = (1.0 - weight) * v + coef * (source[:, lanes] + around)
    last = (SWEEPS - 1) % 2
    for x in range(CX):
        field_ref[x] = buf[last, x + 11, YO : YO + CY, :]
    flat = field_ref[...].reshape(CX * CY, CZ)
    turned = flat.T
    parts = [p.astype(BF16) for p in split3(turned)]
    row_at = lax.broadcasted_iota(jnp.int32, (CX * CY, HALF), 0)
    picked = []
    for k in range(6):
        cell = cell_ref[k : k + 1, :]
        hot = jnp.where(row_at == (cell >> 8), 1.0, 0.0).astype(BF16)
        at_rows = sum(jnp.dot(p, hot, preferred_element_type=F32) for p in parts)
        kept = jnp.where(row_at == (cell & 255), at_rows, 0.0)
        picked.append(jnp.sum(kept, axis=0, keepdims=True))
    sub = lax.broadcasted_iota(jnp.int32, (HALF, HALF), 0)
    tile = jnp.zeros((HALF, HALF), F32)
    for k in range(6):
        tile = jnp.where(sub == k, picked[k], tile)
    turned_tile = tile.T
    both = turned_tile[0:64] + pltpu.roll(turned_tile[64:128], 6, 1)
    traces = pltpu.roll(both, CAP, 1)
    lanes = 3 * CAP
    full = base_ref[...] + traces[:, :lanes]
    for q in range(4):
        msg_ref[q] = full


def first_solve(place, sx, below, above, cells, base):
    return pl.pallas_call(
        first_kernel,
        out_shape=(shaped(CX, CY, CZ), shaped(4, 64, 3 * CAP)),
        in_specs=[SMEM] + [VMEM] * 5,
        out_specs=(VMEM, VMEM),
        scratch_shapes=[pltpu.VMEM((XS, YE, CZ), F32), pltpu.VMEM((2, XS, YE, CZ), F32)],
        compiler_params=PARAMS,
        name="first_solve",
    )(place, sx, below, above, cells, base)


def place_kernel(place_ref, got_ref, out_ref):
    row = place_ref[1]
    got = got_ref[...]
    at = (lax.broadcasted_iota(jnp.int32, (256, 384), 1) + row * 384).astype(F32)
    acc = jnp.zeros((256, 384), F32)
    for i in range(CAP):
        slot = got[:, i : i + 1]
        trace = got[:, CAP + i : CAP + i + 1]
        acc = acc + jnp.where(at == slot, trace, 0.0)
    total = jnp.sum(acc, axis=0, keepdims=True)
    out_ref[...] = jnp.broadcast_to(total[None], (64, 1, 384))


def place_quarter(place, got):
    return pl.pallas_call(
        place_kernel,
        out_shape=shaped(64, 1, 384),
        in_specs=[SMEM, VMEM],
        out_specs=VMEM,
        compiler_params=PARAMS,
        name="place_quarter",
    )(place, got)


SRC = 24576
BLOCK = 1536
QUARTER = 384
CHUNK = 768
TILE = 128


def stack_six(v, order):
    parts = split3(v)
    return jnp.concatenate([parts[i] for i in order], axis=0)


RIGHT = (0, 1, 2, 0, 1, 0)
LEFT = (0, 0, 0, 1, 1, 2)


def prepare_kernel(place_ref, position_ref, moment_ref, right_ref, face_ref, order_ref):
    row = place_ref[1]
    sub = lax.broadcasted_iota(jnp.int32, (8, QUARTER), 0)
    order_ref[...] = jnp.zeros((8, HALF), F32)

    def sources(b, carry):
        node = pl.multiple_of(b * BLOCK + row * QUARTER, HALF)
        at = pl.multiple_of(b * QUARTER, HALF)
        pos = position_ref[:, pl.ds(node, QUARTER)] - 4.0
        mom = moment_ref[:, pl.ds(node, QUARTER)]
        norm = jnp.sum(pos * pos, axis=0, keepdims=True)
        across = jnp.sum(pos * mom, axis=0, keepdims=True)
        dist = jnp.where(sub == 3, 1.0, jnp.where(sub == 4, norm, 0.0))
        face = jnp.where(sub == 4, -across, 0.0)
        for i in range(3):
            dist = jnp.where(sub == i, -2.0 * pos[i : i + 1], dist)
            face = jnp.where(sub == i, mom[i : i + 1], face)
        right_ref[:, pl.ds(at, QUARTER)] = stack_six(dist, RIGHT).astype(BF16)
        face_ref[:, pl.ds(at, QUARTER)] = face
        return carry

    lax.fori_loop(0, SRC // QUARTER, sources, 0, unroll=2)


def prepare(place, position, moment):
    return pl.pallas_call(
        prepare_kernel,
        out_shape=(
            shaped(48, SRC, dtype=BF16),
            shaped(8, SRC),
            shaped(8, HALF),
        ),
        in_specs=[SMEM, VMEM, VMEM],
        out_specs=(VMEM,) * 3,
        compiler_params=PARAMS,
        name="prepare",
    )(place, position, moment)


def targets_kernel(target_ref, left_ref):
    sub = lax.broadcasted_iota(jnp.int32, (8, TILE), 0)
    for t in range(BLOCK // TILE):
        pos = target_ref[:, t * TILE : (t + 1) * TILE] - 4.0
        norm = jnp.sum(pos * pos, axis=0, keepdims=True) + SOFTENING
        feat = jnp.where(sub == 3, norm, jnp.where(sub == 4, 1.0, 0.0))
        for i in range(3):
            feat = jnp.where(sub == i, pos[i : i + 1], feat)
        rows = jnp.concatenate([stack_six(feat, LEFT), jnp.zeros((HALF - 48, TILE), F32)], axis=0)
        left_ref[t * TILE : (t + 1) * TILE, :] = rows.T[:, :48].astype(BF16)


def prepare_targets(targets):
    return pl.pallas_call(
        targets_kernel,
        out_shape=shaped(BLOCK, 48, dtype=BF16),
        in_specs=[VMEM],
        out_specs=VMEM,
        compiler_params=PARAMS,
        name="prepare_targets",
    )(targets)


def layer_kernel(place_ref, left_ref, right_ref, moment_ref, trace_ref, fraction_ref, out_ref, acc):
    brick, row = place_ref[0], place_ref[1]
    acc[...] = jnp.zeros_like(acc)

    def chunk(c, carry):
        at = pl.multiple_of(c * CHUNK, CHUNK)
        trace = jnp.concatenate(
            [trace_ref[pl.ds(2 * c, 1), :], trace_ref[pl.ds(2 * c + 1, 1), :]], axis=1
        )
        face = moment_ref[:, pl.ds(at, CHUNK)] * trace
        face = stack_six(face, RIGHT).astype(BF16)
        dist = right_ref[:, pl.ds(at, CHUNK)]
        for t in range(1536 // TILE):
            rows = slice(t * TILE, (t + 1) * TILE)
            left = left_ref[rows, :]
            total = acc[rows, :]
            for n in range(CHUNK // 256):
                lanes = slice(n * 256, (n + 1) * 256)
                d = jnp.dot(left, dist[:, lanes], preferred_element_type=F32)
                f = jnp.dot(left, face[:, lanes], preferred_element_type=F32)
                r = lax.rsqrt(d)
                term = (f * r) * (r * r)
                total = total + term[:, :HALF] + term[:, HALF:]
            acc[rows, :] = total
        return carry

    lax.fori_loop(0, SRC // CHUNK, chunk, 0)
    for t in range(1536 // TILE):
        turned = acc[t * TILE : (t + 1) * TILE, :].T
        total = jnp.sum(turned, axis=0, keepdims=True)
        out_ref[:, t * TILE : (t + 1) * TILE] = total * (1.0 / (4.0 * math.pi))
    at = pl.multiple_of(row * 384, 128)
    own = (fraction_ref[...] - 1.0) * trace_ref[pl.ds(brick, 1), :]
    out_ref[:, pl.ds(at, 384)] = out_ref[:, pl.ds(at, 384)] + own


def layer(place, left, right, moment, traces, fraction):
    return pl.pallas_call(
        layer_kernel,
        out_shape=shaped(1, 1536),
        in_specs=[SMEM] + [VMEM] * 5,
        out_specs=VMEM,
        scratch_shapes=[pltpu.VMEM((1536, HALF), F32)],
        compiler_params=PARAMS,
        name="layer",
    )(place, left, right, moment, traces, fraction)


def answer_kernel(place_ref, part_ref, got_ref, out_ref, wide, table):
    row = place_ref[1]
    total = jnp.sum(part_ref[...], axis=0, keepdims=True)
    wide[...] = jnp.zeros_like(wide)
    lane = lax.broadcasted_iota(jnp.int32, (256, HALF), 1)
    wide[:, 0 : 3 * CAP] = got_ref[...]
    got = wide[...]
    slot = got.astype(jnp.int32)
    upper, lower = slot >> 7, slot & 127
    value = jnp.zeros((256, HALF), F32)
    for h in range(1536 // HALF):
        entry = jnp.broadcast_to(total[:, h * HALF : (h + 1) * HALF], (256, HALF))
        found = jnp.take_along_axis(entry, lower, axis=1)
        value = jnp.where(upper == h, found, value)
    cell = pltpu.roll(got, HALF - CAP, 1)
    pair = jnp.where(lane < CAP, value, jnp.where(lane < 2 * CAP, cell, 0.0))
    lane80 = lax.broadcasted_iota(jnp.int32, (80, HALF), 1)
    dead = jnp.where((lane80 >= CAP) & (lane80 < 2 * CAP), -1.0, 0.0)
    for q in range(6):
        table[q] = dead
    for q in range(4):
        table[q + 1, 8:72, :] = pair[q * 64 : (q + 1) * 64]
    for t in range(3):
        acc = jnp.zeros((64, HALF), F32)
        for s in range(5):
            piece = table[row + t, 6 + s : 70 + s, :]
            if s > 0:
                piece = pltpu.roll(piece, 2 * CAP * s, 1)
            acc = acc + piece
        out_ref[:, t * HALF : (t + 1) * HALF] = acc


def answer(place, partial, got):
    return pl.pallas_call(
        answer_kernel,
        out_shape=shaped(64, 384),
        in_specs=[SMEM, VMEM, VMEM],
        out_specs=VMEM,
        scratch_shapes=[pltpu.VMEM((256, HALF), F32), pltpu.VMEM((6, 80, HALF), F32)],
        compiler_params=PARAMS,
        name="answer",
    )(place, partial, got)


def second_kernel(place_ref, got_ref, first_ref, out_ref, mask, buf):
    brick, row = place_ref[0], place_ref[1]
    cells_x, cells_y = place_ref[2], place_ref[3]
    buf[0] = jnp.zeros((XD, YE, CZ), F32)
    z_at = lax.broadcasted_iota(jnp.int32, (CZ, HALF), 0)
    for t in range(3):
        block = got_ref[:, t * HALF : (t + 1) * HALF]
        turned = jnp.concatenate([block, pltpu.roll(block, HALF - 6, 1)], axis=0).T
        rows, begin = ((16, 0), (40, 8), (16, 40))[t]
        for s in range(5):
            planes, first_plane = ((4, 0), (8, 4), (8, 12), (8, 20), (4, 28))[s]
            x_off = 4 if s == 0 else 0
            hots, highs, lows = [], [], []
            row_at = lax.broadcasted_iota(jnp.int32, (planes * rows, HALF), 0)
            for k in range(6):
                value = turned[24 * s + k : 24 * s + k + 1, :]
                cell = turned[24 * s + CAP + k : 24 * s + CAP + k + 1, :].astype(jnp.int32)
                x = (cell >> 13) - x_off
                y = (cell >> 8) & 31
                live = (cell >= 0) & (x >= 0) & (x < planes)
                if t == 0:
                    live = live & (y >= 20)
                    y = y - 20
                else:
                    y = y + 4
                    if t == 2:
                        live = live & (y < 16)
                at = jnp.where(live, x * rows + y, -1)
                value = jnp.where(jnp.abs(value) < TINY, TINY, value)
                high = value.astype(BF16).astype(F32)
                hit = z_at == (cell & 255)
                hots.append(jnp.where(row_at == at, 1.0, 0.0).astype(BF16))
                highs.append(jnp.where(hit, high, 0.0).astype(BF16))
                lows.append(jnp.where(hit, value - high, 0.0).astype(BF16))
            hot = jnp.concatenate(hots, axis=1)
            total = None
            for part in (highs, lows):
                term = lax.dot_general(
                    hot, jnp.concatenate(part, axis=1), (((1,), (1,)), ((), ())), preferred_element_type=F32
                )
                total = term if total is None else total + term
            target = buf.at[0, first_plane : first_plane + planes, begin : begin + rows, :]
            target[...] = target[...] + total.reshape(planes, rows, CZ)
    y_at = lax.broadcasted_iota(jnp.int32, (YE, CZ), 0) + (row * CY - YO)
    in_y = (y_at >= 0) & (y_at < cells_y)

    def begin_plane(x, carry):
        v = buf[0, x]
        at = brick * CX + x - YO
        in_x = jnp.where((at >= 0) & (at < cells_x), 1.0, 0.0).astype(F32)
        mask[x] = jnp.where(in_y & (v == 0.0), in_x, 0.0)
        buf[0, x] = jnp.where(jnp.abs(v) < 2.0 * TINY, 0.0, v)
        return carry

    lax.fori_loop(0, XD, begin_plane, 0)
    for k in range(1, SWEEPS + 1):
        weight = WEIGHTS[k - 1]
        src, dst = buf.at[(k - 1) % 2], buf.at[k % 2]

        for x in range(k, XD - k):
            rows = plane_rows(SWEEPS - k - beside(x, YO, CX))
            begin, end = rows
            free = mask[x, begin:end, :]
            for h, (v, around) in enumerate(neighbours(src, x, rows)):
                lanes = slice(h * HALF, (h + 1) * HALF)
                dst[x, begin:end, lanes] = v + free[:, lanes] * ((weight / 6.0) * around - weight * v)
    for x in range(CX):
        out_ref[x] = first_ref[x] + buf[SWEEPS % 2, x + YO, YO : YO + CY, :]


def second_solve(place, got, first):
    return pl.pallas_call(
        second_kernel,
        out_shape=shaped(CX, CY, CZ),
        in_specs=[SMEM, VMEM, VMEM],
        out_specs=VMEM,
        scratch_shapes=[pltpu.VMEM((XD, YE, CZ), F32), pltpu.VMEM((2, XD, YE, CZ), F32)],
        compiler_params=PARAMS,
        name="second_solve",
    )(place, got, first)


def shifted(x, axis, step):
    count = lax.axis_size(axis)
    pairs = [(i, i + step) for i in range(count) if 0 <= i + step < count]
    return lax.ppermute(x, axis, pairs)


def local(
    magnet, node_position, node_moment, solid_fraction, request_cell, request_slot, request_count
):
    bricks, rows = lax.axis_size("brick"), lax.axis_size("row")
    brick, row = lax.axis_index("brick"), lax.axis_index("row")
    place = jnp.stack([brick, row, jnp.int32(bricks * CX), jnp.int32(rows * CY)]).astype(jnp.int32)
    cell, slot = request_cell[0, 0], request_slot[0, 0]
    live = jnp.arange(CAP)[None, :] < request_count[0, 0][:, None]
    zeros = jnp.zeros((bricks, CAP), F32)
    slot_f = jnp.where(live, slot, DEAD_SLOT).astype(F32)
    cell_f = jnp.where(live, cell, -1).astype(F32)
    base = jnp.concatenate([slot_f, zeros, cell_f], axis=1)
    cells = cell.T.reshape(2, 6, bricks).transpose(1, 0, 2).reshape(6, 2 * bricks)
    fraction = lax.dynamic_slice_in_dim(solid_fraction, brick * 1536 + row * 384, 384, 0)[None]
    right, moment, order = prepare(place, node_position, node_moment)
    targets = lax.dynamic_slice_in_dim(node_position, brick * BLOCK, BLOCK, 1)
    left = prepare_targets(targets)

    own, flat, low, high = own_source(magnet)
    l1, r1 = shifted(flat, "brick", 1), shifted(flat, "brick", -1)
    l2, r2 = shifted(high, "brick", 2), shifted(low, "brick", -2)
    sx, upper, lower = join_x(own, l1, r1, l2, r2, order)
    below, above = shifted(upper, "row", 1), shifted(lower, "row", -1)
    first, message = first_solve(place, sx, below, above, cells, base)
    message = message.reshape(rows * bricks, 3 * CAP)
    got = lax.all_to_all(message, ("row", "brick"), split_axis=0, concat_axis=0, tiled=True)
    quarter = place_quarter(place, got)
    traces = lax.all_to_all(quarter, "brick", split_axis=0, concat_axis=0, tiled=True)
    traces = traces.reshape(bricks, QUARTER)
    partial = layer(place, left, right, moment, traces, fraction)
    partials = lax.all_gather(partial, "row", axis=0, tiled=True)
    reply = answer(place, partials, got)
    returned = lax.all_to_all(reply, "brick", split_axis=0, concat_axis=0, tiled=True)
    potential = second_solve(place, returned, first)
    begin = HALF + 2 * 2 * CAP
    boundary = jnp.where(live, returned[:, begin : begin + CAP], 0.0)
    return potential, boundary[None, None]


def solution(mesh):
    placed = (
        P(None, "brick", "row", None),
        P(),
        P(),
        P(),
        P("brick", "row", None, None),
        P("brick", "row", None, None),
        P("brick", "row", None),
    )
    return jax.shard_map(
        local,
        mesh=mesh,
        in_specs=placed,
        out_specs=(P("brick", "row", None), P("brick", "row", None, None)),
        check_vma=False,
    )
```

```python
import functools
import math

import jax
import jax.numpy as jnp
from jax import lax
from jax.experimental import pallas as pl
from jax.experimental.pallas import tpu as pltpu
from jax.sharding import PartitionSpec as P

CX = 8
CY = 32
CZ = 256
SWEEPS = 12
CAP = 12
RELAX_LOW = 0.5
RELAX_HIGH = 2.0
SOFTENING = 0.5

YO = 12
YE = CY + 24
XS = CX + 22
XD = CX + 24
HALF = 128
RIM = CY + 2
PARAMS = pltpu.CompilerParams(vmem_limit_bytes=50 * 1024 * 1024)
DEAD_SLOT = 4096
TINY = 1e-30
F32 = jnp.float32
BF16 = jnp.bfloat16
VMEM = pl.BlockSpec(memory_space=pltpu.VMEM)
SMEM = pl.BlockSpec(memory_space=pltpu.SMEM)


def sweep_weights(total_steps):
    centre = 0.5 * (RELAX_HIGH + RELAX_LOW)
    radius = 0.5 * (RELAX_HIGH - RELAX_LOW)
    root_list = [
        1.0 / (centre + radius * math.cos(math.pi * (2 * order_index + 1) / (2 * total_steps)))
        for order_index in range(total_steps)
    ]
    ordered = []
    for order_index in range(total_steps // 2):
        ordered.append(root_list[order_index])
        ordered.append(root_list[total_steps - 1 - order_index])
    return ordered


WEIGHTS = sweep_weights(SWEEPS)


def shaped(*dims, dtype=F32):
    return jax.ShapeDtypeStruct(dims, dtype)


def split3(v):
    hi = v.astype(BF16).astype(F32)
    rest = v - hi
    mid = rest.astype(BF16).astype(F32)
    return hi, mid, rest - mid


def z_pair(left, right):
    lane = lax.broadcasted_iota(jnp.int32, left.shape, 1)
    left_dn = pltpu.roll(left, 1, 1)
    right_dn = pltpu.roll(right, 1, 1)
    left_up = pltpu.roll(left, HALF - 1, 1)
    right_up = pltpu.roll(right, HALF - 1, 1)
    first, last = lane == 0, lane == HALF - 1
    dn = (jnp.where(first, 0.0, left_dn), jnp.where(first, left_dn, right_dn))
    up = (jnp.where(last, right_up, left_up), jnp.where(last, 0.0, right_up))
    return dn, up


def source_kernel(m_ref, e_ref, flat_ref, low_ref, high_ref, pad):
    pad[...] = jnp.zeros_like(pad)
    for x in range(CX):
        pad[0, x + 1, 12:44, :] = m_ref[0, x]
        pad[1, x + 1, 12:44, :] = m_ref[1, x]
        pad[2, x + 1, 12:44, :] = m_ref[2, x]
    zeros = jnp.zeros((40, CZ), F32)
    for i in range(CX + 2):
        ahead = pad[0, i + 1, 8:48, :] if i + 1 <= CX else zeros
        behind = pad[0, i - 1, 8:48, :] if i >= 2 else zeros
        total = ahead - behind
        if 1 <= i <= CX:
            total = total + (pad[1, i, 9:49, :] - pad[1, i, 7:47, :])
            c = pad[2, i, 8:48, :]
            dn, up = z_pair(c[:, :HALF], c[:, HALF:])
            total = total + jnp.concatenate([up[0] - dn[0], up[1] - dn[1]], axis=1)
        total = -0.5 * total
        e_ref[i] = total
        rim = e_ref[i, 3:37, :]
        flat_ref[i * RIM : (i + 1) * RIM, :] = rim
        if i < 4:
            low_ref[i * RIM : (i + 1) * RIM, :] = rim
        j = i - (CX - 2)
        if j >= 0:
            high_ref[j * RIM : (j + 1) * RIM, :] = rim


def own_source(magnet):
    return pl.pallas_call(
        source_kernel,
        out_shape=(
            shaped(10, 40, CZ),
            shaped(10 * RIM, CZ),
            shaped(4 * RIM, CZ),
            shaped(4 * RIM, CZ),
        ),
        in_specs=[VMEM],
        out_specs=(VMEM,) * 4,
        scratch_shapes=[pltpu.VMEM((3, CX + 2, 56, CZ), F32)],
        compiler_params=PARAMS,
        name="own_source",
    )(magnet)


def beside(plane, before, own):
    return max(before - plane, plane - (before + own - 1), 0)


def y_rows():
    counts = [CX + 4 - beside(plane, 11, CX) for plane in range(XS)]
    begins = [sum(counts[:plane]) for plane in range(XS)]
    return counts, begins, -(-sum(counts) // 8) * 8


Y_COUNTS, Y_BEGINS, Y_TOTAL = y_rows()


def join_kernel(e_ref, l1_ref, r1_ref, l2_ref, r2_ref, order_ref, sx_ref, upper_ref, lower_ref):
    del order_ref
    parts = ((l1_ref, 2, 10), (r1_ref, 18, 10), (l2_ref, 0, 4), (r2_ref, 26, 4))
    upper_ref[Y_TOTAL - 8 :, :] = jnp.zeros((8, CZ), F32)
    lower_ref[Y_TOTAL - 8 :, :] = jnp.zeros((8, CZ), F32)
    for plane in range(XS):
        own = 10 <= plane < 20
        sx_ref[plane] = e_ref[plane - 10] if own else jnp.zeros((40, CZ), F32)
        total = sx_ref[plane, 3:37, :] if own else None
        for ref, begin, count in parts:
            if begin <= plane < begin + count:
                at = (plane - begin) * RIM
                term = ref[at : at + RIM, :]
                total = term if total is None else total + term
        sx_ref[plane, 3:37, :] = total
        rows, at = Y_COUNTS[plane], Y_BEGINS[plane]
        upper_ref[at : at + rows, :] = sx_ref[plane, 37 - rows : 37, :]
        lower_ref[at : at + rows, :] = sx_ref[plane, 3 : 3 + rows, :]


def join_x(own, l1, r1, l2, r2, order):
    return pl.pallas_call(
        join_kernel,
        out_shape=(shaped(XS, 40, CZ), shaped(Y_TOTAL, CZ), shaped(Y_TOTAL, CZ)),
        in_specs=[VMEM] * 6,
        out_specs=(VMEM,) * 3,
        compiler_params=PARAMS,
        name="join_x",
    )(own, l1, r1, l2, r2, order)


def plane_rows(reach):
    return (0, YE) if reach > 3 else (8, YE - 8)


def neighbours(src, x, rows):
    begin, end = rows
    c = src[x, begin:end, :]
    around_x = src[x - 1, begin:end, :] + src[x + 1, begin:end, :]
    halves = (c[:, :HALF], c[:, HALF:])
    dn, up = z_pair(*halves)
    out = []
    for h in range(2):
        v = halves[h]
        around_y = pltpu.roll(v, 1, 0) + pltpu.roll(v, end - begin - 1, 0)
        around = around_x[:, h * HALF : (h + 1) * HALF] + around_y + (dn[h] + up[h])
        out.append((v, around))
    return out


def first_kernel(place_ref, sx_ref, below_ref, above_ref, cell_ref, base_ref, field_ref, msg_ref, s, buf):
    brick, row = place_ref[0], place_ref[1]
    cells_x, cells_y = place_ref[2], place_ref[3]
    y_at = lax.broadcasted_iota(jnp.int32, (YE, HALF), 0) + (row * CY - YO)
    in_y = jnp.where((y_at >= 0) & (y_at < cells_y), 1.0, 0.0).astype(F32)

    def x_scale(x, scale):
        at = brick * CX + x - 11
        return jnp.where((at >= 0) & (at < cells_x), scale, 0.0).astype(F32)

    edge = jnp.zeros((8, CZ), F32)
    for x in range(XS):
        s[x, 0:8, :] = edge
        s[x, 48:56, :] = edge
        s[x, 8:48, :] = sx_ref[x]
        rows, at = Y_COUNTS[x], Y_BEGINS[x]
        s[x, 13 - rows : 13, :] += below_ref[at : at + rows, :]
        s[x, 43 : 43 + rows, :] += above_ref[at : at + rows, :]
        coef = in_y * x_scale(x, WEIGHTS[0] / 6.0)
        full = s[x]
        buf[0, x, :, :HALF] = coef * full[:, :HALF]
        buf[0, x, :, HALF:] = coef * full[:, HALF:]
    for k in range(1, SWEEPS):
        weight = WEIGHTS[k]
        src, dst = buf.at[(k - 1) % 2], buf.at[k % 2]

        for x in range(k, XS - k):
            rows = plane_rows(SWEEPS - 1 - k - beside(x, 11, CX))
            begin, end = rows
            coef = in_y[begin:end] * x_scale(x, weight / 6.0)
            source = s[x, begin:end, :]
            for h, (v, around) in enumerate(neighbours(src, x, rows)):
                lanes = slice(h * HALF, (h + 1) * HALF)
                dst[x, begin:end, lanes] = (1.0 - weight) * v + coef * (source[:, lanes] + around)
    last = (SWEEPS - 1) % 2
    for x in range(CX):
        field_ref[x] = buf[last, x + 11, YO : YO + CY, :]
    flat = field_ref[...].reshape(CX * CY, CZ)
    turned = flat.T
    parts = [p.astype(BF16) for p in split3(turned)]
    row_at = lax.broadcasted_iota(jnp.int32, (CX * CY, HALF), 0)
    picked = []
    for k in range(6):
        cell = cell_ref[k : k + 1, :]
        hot = jnp.where(row_at == (cell >> 8), 1.0, 0.0).astype(BF16)
        at_rows = sum(jnp.dot(p, hot, preferred_element_type=F32) for p in parts)
        kept = jnp.where(row_at == (cell & 255), at_rows, 0.0)
        picked.append(jnp.sum(kept, axis=0, keepdims=True))
    sub = lax.broadcasted_iota(jnp.int32, (HALF, HALF), 0)
    tile = jnp.zeros((HALF, HALF), F32)
    for k in range(6):
        tile = jnp.where(sub == k, picked[k], tile)
    turned_tile = tile.T
    both = turned_tile[0:64] + pltpu.roll(turned_tile[64:128], 6, 1)
    traces = pltpu.roll(both, CAP, 1)
    lanes = 3 * CAP
    full = base_ref[...] + traces[:, :lanes]
    for q in range(4):
        msg_ref[q] = full


def first_solve(place, sx, below, above, cells, base):
    return pl.pallas_call(
        first_kernel,
        out_shape=(shaped(CX, CY, CZ), shaped(4, 64, 3 * CAP)),
        in_specs=[SMEM] + [VMEM] * 5,
        out_specs=(VMEM, VMEM),
        scratch_shapes=[pltpu.VMEM((XS, YE, CZ), F32), pltpu.VMEM((2, XS, YE, CZ), F32)],
        compiler_params=PARAMS,
        name="first_solve",
    )(place, sx, below, above, cells, base)


def place_kernel(place_ref, got_ref, out_ref):
    row = place_ref[1]
    got = got_ref[...]
    at = (lax.broadcasted_iota(jnp.int32, (256, 384), 1) + row * 384).astype(F32)
    acc = jnp.zeros((256, 384), F32)
    for i in range(CAP):
        slot = got[:, i : i + 1]
        trace = got[:, CAP + i : CAP + i + 1]
        acc = acc + jnp.where(at == slot, trace, 0.0)
    total = jnp.sum(acc, axis=0, keepdims=True)
    out_ref[...] = jnp.broadcast_to(total[None], (64, 1, 384))


def place_quarter(place, got):
    return pl.pallas_call(
        place_kernel,
        out_shape=shaped(64, 1, 384),
        in_specs=[SMEM, VMEM],
        out_specs=VMEM,
        compiler_params=PARAMS,
        name="place_quarter",
    )(place, got)


SRC = 24576
BLOCK = 1536
QUARTER = 384
CHUNK = 768
TILE = 128


def stack_six(v, order):
    parts = split3(v)
    return jnp.concatenate([parts[i] for i in order], axis=0)


RIGHT = (0, 1, 2, 0, 1, 0)
LEFT = (0, 0, 0, 1, 1, 2)


def prepare_kernel(place_ref, position_ref, moment_ref, right_ref, face_ref, order_ref):
    row = place_ref[1]
    sub = lax.broadcasted_iota(jnp.int32, (8, QUARTER), 0)
    order_ref[...] = jnp.zeros((8, HALF), F32)

    def sources(b, carry):
        node = pl.multiple_of(b * BLOCK + row * QUARTER, HALF)
        at = pl.multiple_of(b * QUARTER, HALF)
        pos = position_ref[:, pl.ds(node, QUARTER)] - 4.0
        mom = moment_ref[:, pl.ds(node, QUARTER)]
        norm = jnp.sum(pos * pos, axis=0, keepdims=True)
        across = jnp.sum(pos * mom, axis=0, keepdims=True)
        dist = jnp.where(sub == 3, 1.0, jnp.where(sub == 4, norm, 0.0))
        face = jnp.where(sub == 4, -across, 0.0)
        for i in range(3):
            dist = jnp.where(sub == i, -2.0 * pos[i : i + 1], dist)
            face = jnp.where(sub == i, mom[i : i + 1], face)
        right_ref[:, pl.ds(at, QUARTER)] = stack_six(dist, RIGHT).astype(BF16)
        face_ref[:, pl.ds(at, QUARTER)] = face
        return carry

    lax.fori_loop(0, SRC // QUARTER, sources, 0, unroll=2)


def prepare(place, position, moment):
    return pl.pallas_call(
        prepare_kernel,
        out_shape=(
            shaped(48, SRC, dtype=BF16),
            shaped(8, SRC),
            shaped(8, HALF),
        ),
        in_specs=[SMEM, VMEM, VMEM],
        out_specs=(VMEM,) * 3,
        compiler_params=PARAMS,
        name="prepare",
    )(place, position, moment)


def targets_kernel(target_ref, left_ref):
    sub = lax.broadcasted_iota(jnp.int32, (8, TILE), 0)
    for t in range(BLOCK // TILE):
        pos = target_ref[:, t * TILE : (t + 1) * TILE] - 4.0
        norm = jnp.sum(pos * pos, axis=0, keepdims=True) + SOFTENING
        feat = jnp.where(sub == 3, norm, jnp.where(sub == 4, 1.0, 0.0))
        for i in range(3):
            feat = jnp.where(sub == i, pos[i : i + 1], feat)
        rows = jnp.concatenate([stack_six(feat, LEFT), jnp.zeros((HALF - 48, TILE), F32)], axis=0)
        left_ref[t * TILE : (t + 1) * TILE, :] = rows.T[:, :48].astype(BF16)


def prepare_targets(targets):
    return pl.pallas_call(
        targets_kernel,
        out_shape=shaped(BLOCK, 48, dtype=BF16),
        in_specs=[VMEM],
        out_specs=VMEM,
        compiler_params=PARAMS,
        name="prepare_targets",
    )(targets)


def layer_kernel(place_ref, left_ref, right_ref, moment_ref, trace_ref, fraction_ref, out_ref, acc):
    brick, row = place_ref[0], place_ref[1]
    acc[...] = jnp.zeros_like(acc)

    def chunk(c, carry):
        at = pl.multiple_of(c * CHUNK, CHUNK)
        trace = jnp.concatenate(
            [trace_ref[pl.ds(2 * c, 1), :], trace_ref[pl.ds(2 * c + 1, 1), :]], axis=1
        )
        face = moment_ref[:, pl.ds(at, CHUNK)] * trace
        face = stack_six(face, RIGHT).astype(BF16)
        dist = right_ref[:, pl.ds(at, CHUNK)]
        for t in range(1536 // TILE):
            rows = slice(t * TILE, (t + 1) * TILE)
            left = left_ref[rows, :]
            total = acc[rows, :]
            for n in range(CHUNK // 256):
                lanes = slice(n * 256, (n + 1) * 256)
                d = jnp.dot(left, dist[:, lanes], preferred_element_type=F32)
                f = jnp.dot(left, face[:, lanes], preferred_element_type=F32)
                r = lax.rsqrt(d)
                term = (f * r) * (r * r)
                total = total + term[:, :HALF] + term[:, HALF:]
            acc[rows, :] = total
        return carry

    lax.fori_loop(0, SRC // CHUNK, chunk, 0, unroll=2)
    for t in range(1536 // TILE):
        turned = acc[t * TILE : (t + 1) * TILE, :].T
        total = jnp.sum(turned, axis=0, keepdims=True)
        out_ref[:, t * TILE : (t + 1) * TILE] = total * (1.0 / (4.0 * math.pi))
    at = pl.multiple_of(row * 384, 128)
    own = (fraction_ref[...] - 1.0) * trace_ref[pl.ds(brick, 1), :]
    out_ref[:, pl.ds(at, 384)] = out_ref[:, pl.ds(at, 384)] + own


def layer(place, left, right, moment, traces, fraction):
    return pl.pallas_call(
        layer_kernel,
        out_shape=shaped(1, 1536),
        in_specs=[SMEM] + [VMEM] * 5,
        out_specs=VMEM,
        scratch_shapes=[pltpu.VMEM((1536, HALF), F32)],
        compiler_params=PARAMS,
        name="layer",
    )(place, left, right, moment, traces, fraction)


def answer_kernel(place_ref, part_ref, got_ref, out_ref, wide, table):
    row = place_ref[1]
    total = jnp.sum(part_ref[...], axis=0, keepdims=True)
    wide[...] = jnp.zeros_like(wide)
    lane = lax.broadcasted_iota(jnp.int32, (256, HALF), 1)
    wide[:, 0 : 3 * CAP] = got_ref[...]
    got = wide[...]
    slot = got.astype(jnp.int32)
    upper, lower = slot >> 7, slot & 127
    value = jnp.zeros((256, HALF), F32)
    for h in range(1536 // HALF):
        entry = jnp.broadcast_to(total[:, h * HALF : (h + 1) * HALF], (256, HALF))
        found = jnp.take_along_axis(entry, lower, axis=1)
        value = jnp.where(upper == h, found, value)
    cell = pltpu.roll(got, HALF - CAP, 1)
    pair = jnp.where(lane < CAP, value, jnp.where(lane < 2 * CAP, cell, 0.0))
    lane80 = lax.broadcasted_iota(jnp.int32, (80, HALF), 1)
    dead = jnp.where((lane80 >= CAP) & (lane80 < 2 * CAP), -1.0, 0.0)
    for q in range(6):
        table[q] = dead
    for q in range(4):
        table[q + 1, 8:72, :] = pair[q * 64 : (q + 1) * 64]
    for t in range(3):
        acc = jnp.zeros((64, HALF), F32)
        for s in range(5):
            piece = table[row + t, 6 + s : 70 + s, :]
            if s > 0:
                piece = pltpu.roll(piece, 2 * CAP * s, 1)
            acc = acc + piece
        out_ref[:, t * HALF : (t + 1) * HALF] = acc


def answer(place, partial, got):
    return pl.pallas_call(
        answer_kernel,
        out_shape=shaped(64, 384),
        in_specs=[SMEM, VMEM, VMEM],
        out_specs=VMEM,
        scratch_shapes=[pltpu.VMEM((256, HALF), F32), pltpu.VMEM((6, 80, HALF), F32)],
        compiler_params=PARAMS,
        name="answer",
    )(place, partial, got)


def second_kernel(place_ref, got_ref, first_ref, out_ref, mask, buf):
    brick, row = place_ref[0], place_ref[1]
    cells_x, cells_y = place_ref[2], place_ref[3]
    buf[0] = jnp.zeros((XD, YE, CZ), F32)
    z_at = lax.broadcasted_iota(jnp.int32, (CZ, HALF), 0)
    for t in range(3):
        block = got_ref[:, t * HALF : (t + 1) * HALF]
        turned = jnp.concatenate([block, pltpu.roll(block, HALF - 6, 1)], axis=0).T
        rows, begin = ((16, 0), (40, 8), (16, 40))[t]
        for s in range(5):
            planes, first_plane = ((4, 0), (8, 4), (8, 12), (8, 20), (4, 28))[s]
            x_off = 4 if s == 0 else 0
            hots, highs, lows = [], [], []
            row_at = lax.broadcasted_iota(jnp.int32, (planes * rows, HALF), 0)
            for k in range(6):
                value = turned[24 * s + k : 24 * s + k + 1, :]
                cell = turned[24 * s + CAP + k : 24 * s + CAP + k + 1, :].astype(jnp.int32)
                x = (cell >> 13) - x_off
                y = (cell >> 8) & 31
                live = (cell >= 0) & (x >= 0) & (x < planes)
                if t == 0:
                    live = live & (y >= 20)
                    y = y - 20
                else:
                    y = y + 4
                    if t == 2:
                        live = live & (y < 16)
                at = jnp.where(live, x * rows + y, -1)
                value = jnp.where(jnp.abs(value) < TINY, TINY, value)
                high = value.astype(BF16).astype(F32)
                hit = z_at == (cell & 255)
                hots.append(jnp.where(row_at == at, 1.0, 0.0).astype(BF16))
                highs.append(jnp.where(hit, high, 0.0).astype(BF16))
                lows.append(jnp.where(hit, value - high, 0.0).astype(BF16))
            hot = jnp.concatenate(hots, axis=1)
            total = None
            for part in (highs, lows):
                term = lax.dot_general(
                    hot, jnp.concatenate(part, axis=1), (((1,), (1,)), ((), ())), preferred_element_type=F32
                )
                total = term if total is None else total + term
            target = buf.at[0, first_plane : first_plane + planes, begin : begin + rows, :]
            target[...] = target[...] + total.reshape(planes, rows, CZ)
    y_at = lax.broadcasted_iota(jnp.int32, (YE, CZ), 0) + (row * CY - YO)
    in_y = (y_at >= 0) & (y_at < cells_y)

    def begin_plane(x, carry):
        v = buf[0, x]
        at = brick * CX + x - YO
        in_x = jnp.where((at >= 0) & (at < cells_x), 1.0, 0.0).astype(F32)
        mask[x] = jnp.where(in_y & (v == 0.0), in_x, 0.0)
        buf[0, x] = jnp.where(jnp.abs(v) < 2.0 * TINY, 0.0, v)
        return carry

    lax.fori_loop(0, XD, begin_plane, 0)
    for k in range(1, SWEEPS + 1):
        weight = WEIGHTS[k - 1]
        src, dst = buf.at[(k - 1) % 2], buf.at[k % 2]

        for x in range(k, XD - k):
            rows = plane_rows(SWEEPS - k - beside(x, YO, CX))
            begin, end = rows
            free = mask[x, begin:end, :]
            for h, (v, around) in enumerate(neighbours(src, x, rows)):
                lanes = slice(h * HALF, (h + 1) * HALF)
                dst[x, begin:end, lanes] = v + free[:, lanes] * ((weight / 6.0) * around - weight * v)
    for x in range(CX):
        out_ref[x] = first_ref[x] + buf[SWEEPS % 2, x + YO, YO : YO + CY, :]


def second_solve(place, got, first):
    return pl.pallas_call(
        second_kernel,
        out_shape=shaped(CX, CY, CZ),
        in_specs=[SMEM, VMEM, VMEM],
        out_specs=VMEM,
        scratch_shapes=[pltpu.VMEM((XD, YE, CZ), F32), pltpu.VMEM((2, XD, YE, CZ), F32)],
        compiler_params=PARAMS,
        name="second_solve",
    )(place, got, first)


def shifted(x, axis, step):
    count = lax.axis_size(axis)
    pairs = [(i, i + step) for i in range(count) if 0 <= i + step < count]
    return lax.ppermute(x, axis, pairs)


def local(
    magnet, node_position, node_moment, solid_fraction, request_cell, request_slot, request_count
):
    bricks, rows = lax.axis_size("brick"), lax.axis_size("row")
    brick, row = lax.axis_index("brick"), lax.axis_index("row")
    place = jnp.stack([brick, row, jnp.int32(bricks * CX), jnp.int32(rows * CY)]).astype(jnp.int32)
    cell, slot = request_cell[0, 0], request_slot[0, 0]
    live = jnp.arange(CAP)[None, :] < request_count[0, 0][:, None]
    zeros = jnp.zeros((bricks, CAP), F32)
    slot_f = jnp.where(live, slot, DEAD_SLOT).astype(F32)
    cell_f = jnp.where(live, cell, -1).astype(F32)
    base = jnp.concatenate([slot_f, zeros, cell_f], axis=1)
    cells = cell.T.reshape(2, 6, bricks).transpose(1, 0, 2).reshape(6, 2 * bricks)
    fraction = lax.dynamic_slice_in_dim(solid_fraction, brick * 1536 + row * 384, 384, 0)[None]
    right, moment, order = prepare(place, node_position, node_moment)
    targets = lax.dynamic_slice_in_dim(node_position, brick * BLOCK, BLOCK, 1)
    left = prepare_targets(targets)

    own, flat, low, high = own_source(magnet)
    l1, r1 = shifted(flat, "brick", 1), shifted(flat, "brick", -1)
    l2, r2 = shifted(high, "brick", 2), shifted(low, "brick", -2)
    sx, upper, lower = join_x(own, l1, r1, l2, r2, order)
    below, above = shifted(upper, "row", 1), shifted(lower, "row", -1)
    first, message = first_solve(place, sx, below, above, cells, base)
    message = message.reshape(rows * bricks, 3 * CAP)
    got = lax.all_to_all(message, ("row", "brick"), split_axis=0, concat_axis=0, tiled=True)
    quarter = place_quarter(place, got)
    traces = lax.all_to_all(quarter, "brick", split_axis=0, concat_axis=0, tiled=True)
    traces = traces.reshape(bricks, QUARTER)
    partial = layer(place, left, right, moment, traces, fraction)
    partials = lax.all_gather(partial, "row", axis=0, tiled=True)
    reply = answer(place, partials, got)
    returned = lax.all_to_all(reply, "brick", split_axis=0, concat_axis=0, tiled=True)
    potential = second_solve(place, returned, first)
    begin = HALF + 2 * 2 * CAP
    boundary = jnp.where(live, returned[:, begin : begin + CAP], 0.0)
    return potential, boundary[None, None]


def solution(mesh):
    placed = (
        P(None, "brick", "row", None),
        P(),
        P(),
        P(),
        P("brick", "row", None, None),
        P("brick", "row", None, None),
        P("brick", "row", None),
    )
    return jax.shard_map(
        local,
        mesh=mesh,
        in_specs=placed,
        out_specs=(P("brick", "row", None), P("brick", "row", None, None)),
        check_vma=False,
    )
```
